128 devices in a mesh: dp: 32 (over z_hi, y, x), tensor: 4 (over z_lo, core).
Axes of the slice: x: 4, y: 4, z: 4 (z_hi: 2, z_lo: 2; z = z_hi * 2 + z_lo), core: 2. Of those that a mesh axis runs over, the one named last changes fastest.
Arguments:
- train_act: bfloat16 [128, 128, 5120], P('dp', None, 'tensor'), may hold values from -6 to 6
- train_grad: bfloat16 [128, 128, 5120], P('dp', None, 'tensor'), may hold values from -6 to 6
- val_act: bfloat16 [32, 128, 5120], P('dp', None, 'tensor'), may hold values from -6 to 6
- val_grad: bfloat16 [32, 128, 5120], P('dp', None, 'tensor'), may hold values from -6 to 6
Outputs:
- shapley: float32 [128, 32], P('dp')
The draws below stay inside these ranges and needn't reach their ends.
All inputs are finite; a program needn't handle non-finite values.
Results may differ from the reference program's by a relative error of at most 0.0003.
Values may be sent and summed in bfloat16 or wider, within the bound.
A program may use at most 64 MiB of HBM per device.

```python
import jax
import jax.numpy as jnp
from jax import lax

D = 5120
L = 128
TRAINS = 128
VALS = 32
N_TENSOR = 4


def levels(rng, extent, shards, least, high):
    loudness = 1.0
    for position, blocks in shards:
        steps = jax.random.uniform(jax.random.fold_in(jax.random.fold_in(rng, 6), position), (blocks,), jnp.float32, least / len(shards), high / len(shards))
        loudness = loudness * jnp.repeat(jnp.exp(steps), extent[position] // blocks).reshape((-1,) + (1,) * (len(extent) - 1 - position))
    return loudness


def gaussian(stream_key, shape, spread, reach, cuts=(), held_as=jnp.bfloat16):
    array = jax.random.normal(stream_key, shape, jnp.float32) * spread
    if len(cuts) > 0:
        array = levels(stream_key, shape, cuts, -0.22, 0.18) * array
    return jnp.clip(array, min=-reach, max=reach).astype(held_as)


def setup_inputs(seed: int = 0) -> dict:
    seeds = jax.random.split(jax.random.key(seed), 5)
    train_act = gaussian(seeds[0], (TRAINS, L, D), 1.0, 6.0, ((0, 32), (2, 4)))
    train_grad = gaussian(seeds[1], (TRAINS, L, D), 1.0, 6.0, ((0, 32), (2, 4)))
    val_act = gaussian(seeds[2], (VALS, L, D), 1.0, 6.0, ((0, 32), (2, 4)))
    val_grad = gaussian(seeds[3], (VALS, L, D), 1.0, 6.0, ((0, 32), (2, 4)))
    return {"train_act": train_act, "train_grad": train_grad, "val_act": val_act, "val_grad": val_grad}


def reference(train_act, train_grad, val_act, val_grad):
    width = D // N_TENSOR
    scale = D ** -0.5
    flat_act = train_act.reshape(TRAINS * L, D)
    flat_grad = train_grad.reshape(TRAINS * L, D)

    def one_val(pair):
        va, vg = pair
        act_gram = jnp.zeros((TRAINS * L, L), jnp.float32)
        grad_gram = jnp.zeros((TRAINS * L, L), jnp.float32)
        for k in range(N_TENSOR):
            low = k * width
            high = low + width
            part_act = jnp.dot(flat_act[:, low:high], va[:, low:high].T, preferred_element_type=jnp.float32) * scale
            part_grad = jnp.dot(flat_grad[:, low:high], vg[:, low:high].T, preferred_element_type=jnp.float32) * scale
            act_gram = act_gram + part_act
            grad_gram = grad_gram + part_grad
        product = (act_gram * grad_gram).reshape(TRAINS, L * L)
        return jnp.sum(product, axis=1) / L

    scores = lax.map(one_val, (val_act, val_grad))
    return scores.T
```

```python
import functools

import jax
import jax.numpy as jnp
from jax import lax
from jax.experimental import pallas as pl
from jax.experimental.pallas import tpu as pltpu
from jax.sharding import PartitionSpec as P

MESH = pl.DeviceIdType.MESH
RING = 4


def kernel(
    total_width,
    train_act,
    train_grad,
    val_act,
    val_grad,
    out_ref,
    trains,
    vals,
    grams,
    from_core,
    sums,
    tiles,
    arrived,
    local_sem,
    send_sem,
    recv_sem,
):
    seq_len = train_act.shape[1]
    train_in = (train_act, train_grad)
    val_in = (val_act, val_grad)

    dp = lax.axis_index("dp")
    tensor = lax.axis_index("tensor")
    z_hi, y, x = dp // 16, (dp // 4) % 4, dp % 4
    z_lo, core = tensor // 2, tensor % 2

    def at(z_hi, y, x, z_lo, core):
        return (z_hi * 16 + y * 4 + x, z_lo * 2 + core)

    x_next, x_prev = (x + 1) % 4, (x + 3) % 4
    y_next, y_prev = (y + 1) % 4, (y + 3) % 4
    to_x_next = at(z_hi, y, x_next, z_lo, core)
    to_x_prev = at(z_hi, y, x_prev, z_lo, core)
    to_y_next = at(z_hi, y_next, x, z_lo, core)
    to_y_prev = at(z_hi, y_prev, x, z_lo, core)
    to_lo = at(z_hi, y, x, 1 - z_lo, core)
    to_hi = at(1 - z_hi, y, x, 1 - z_lo, core)
    to_core = at(z_hi, y, x, z_lo, 1 - core)
    x_at = (x, x_prev, x_next, (x + 2) % 4)
    y_at = (y, y_prev, y_next, (y + 2) % 4)

    mine = pl.ds(z_lo * 2, 2)
    theirs = pl.ds((1 - z_lo) * 2, 2)
    local = []
    for m in range(2):
        local.append(
            pltpu.make_async_copy(train_in[m].at[mine], trains.at[m, 0, 0], local_sem.at[m])
        )
        local.append(
            pltpu.make_async_copy(val_in[m], vals.at[m, 0, 0, pl.ds(0, 1)], local_sem.at[2 + m])
        )
    for copy in local:
        copy.start()

    group = [
        (b, d, at(z_hi, y, x_at[b], *((z_lo, core), (z_lo, 1 - core), (1 - z_lo, core), (1 - z_lo, 1 - core))[d]))
        for b in range(RING)
        for d in range(4)
        if (b, d) != (0, 0)
    ]
    barrier = pltpu.get_barrier_semaphore()
    partners = [device for _, _, device in group] + [to_y_next, to_y_prev, to_hi]
    for device in partners:
        pl.semaphore_signal(barrier, inc=1, device_id=device, device_id_type=MESH)
    pl.semaphore_wait(barrier, len(partners))

    copies = {}

    def send(name, src, dst, device):
        key = len(copies)
        copies[name] = pltpu.make_async_remote_copy(
            src_ref=src,
            dst_ref=dst,
            send_sem=send_sem.at[key],
            recv_sem=recv_sem.at[key],
            device_id=device,
            device_id_type=MESH,
        )
        copies[name].start()

    def got(name):
        copies[name].wait_recv()

    def x_direct(s, m):
        src = train_in[m].at[mine] if s == 0 else trains.at[m, 1, 0]
        send(("x", s, m, 1), src, trains.at[m, s, 1], to_x_next)
        send(("x", s, m, 2), src, trains.at[m, s, 2], to_x_prev)

    def x_forward(s, m):
        got(("x", s, m, 1 + m))
        send(("x", s, m, 3), trains.at[m, s, 1 + m], trains.at[m, s, 3], (to_x_next, to_x_prev)[m])

    def x_near(s, m):
        got(("x", s, m, 2 - m))

    def x_far(s, m):
        got(("x", s, m, 3))

    def y_direct(s, w, m):
        src = val_in[m] if (s, w) == (0, 0) else vals.at[m, s, 0, pl.ds(w, 1)]
        send(("y", s, w, m, 1), src, vals.at[m, s, 1, pl.ds(w, 1)], to_y_next)
        send(("y", s, w, m, 2), src, vals.at[m, s, 2, pl.ds(w, 1)], to_y_prev)

    def y_forward(s, w, m):
        got(("y", s, w, m, 1 + m))
        here = vals.at[m, s, 1 + m, pl.ds(w, 1)]
        send(("y", s, w, m, 3), here, vals.at[m, s, 3, pl.ds(w, 1)], (to_y_next, to_y_prev)[m])

    def y_rest(s, w, m):
        got(("y", s, w, m, 2 - m))
        got(("y", s, w, m, 3))

    def gram(s, blocks):
        def one(i, carry):
            v, m = i // 2, i % 2
            for b in blocks:
                left = trains[m, s, b].reshape(2 * seq_len, -1)
                right = vals[m, s, v].reshape(2 * seq_len, -1)
                part = lax.dot_general(
                    left, right, (((1,), (1,)), ((), ())), preferred_element_type=jnp.float32
                )
                for r in range(2):
                    rows = part[r * seq_len : (r + 1) * seq_len]
                    if s == 0:
                        grams[b, v, r, m] = rows
                    else:
                        grams[b, v, r, m] += rows
            return carry

        lax.fori_loop(0, 2 * RING, one, 0)

    for m in range(2):
        send(("lo", m), val_in[m], vals.at[m, 1, 0, pl.ds(0, 1)], to_lo)
        send(("hi", m), val_in[m], vals.at[m, 1, 0, pl.ds(1, 1)], to_hi)
        y_direct(0, 0, m)
        x_direct(0, m)
    for m in range(2):
        send(("swap", m), train_in[m].at[theirs], trains.at[m, 1, 0], to_lo)

    def hand_over(m):
        got(("lo", m))
        send(("far", m), vals.at[m, 1, 0, pl.ds(0, 1)], vals.at[m, 0, 0, pl.ds(1, 1)], to_hi)
        y_direct(1, 0, m)

    def take_hi(m):
        got(("hi", m))
        y_direct(1, 1, m)

    def take_far(m):
        got(("far", m))
        y_direct(0, 1, m)

    def take_swap(m):
        got(("swap", m))
        x_direct(1, m)

    for m in range(2):
        y_forward(0, 0, m)
        hand_over(m)
        take_hi(m)
    x_forward(0, 0)
    x_forward(0, 1)
    take_far(0)
    take_far(1)
    take_swap(0)
    take_swap(1)
    for copy in local:
        copy.wait()
    for m in range(2):
        y_rest(0, 0, m)
    for w, s in ((1, 1), (0, 1), (1, 0)):
        for m in range(2):
            y_forward(s, w, m)
    for m in range(2):
        x_near(0, m)
        x_far(0, m)
        y_rest(0, 1, m)
    x_forward(1, 0)
    gram(0, (0, 1))
    x_forward(1, 1)
    gram(0, (2, 3))
    for m in range(2):
        y_rest(1, 0, m)
        y_rest(1, 1, m)
        x_near(1, m)
    gram(1, (0, 1))
    for m in range(2):
        x_far(1, m)
    gram(1, (2, 3))

    for b in range(RING):
        for v in range(RING):
            send(("core", b, v), grams.at[b, v, 1 - core], from_core.at[b, v], to_core)
    lane = lax.broadcasted_iota(jnp.int32, (8, 128), 1)
    row = lax.broadcasted_iota(jnp.int32, (8, 128), 0)
    sums[...] = jnp.zeros_like(sums)
    for b in range(RING):
        for v in range(RING):
            got(("core", b, v))
            act = grams[b, v, core, 0] + from_core[b, v, 0]
            grad = grams[b, v, core, 1] + from_core[b, v, 1]
            sums[pl.ds(b, 1), pl.ds(v * 2 * seq_len, 2 * seq_len)] = jnp.sum(
                act * grad, axis=0, keepdims=True
            )
    scores = jnp.zeros((8, 128), jnp.float32)
    for v in range(RING):
        for w in range(2):
            first = (v * 2 + w) * seq_len
            one = jnp.sum(sums[:, first : first + seq_len], axis=1, keepdims=True)
            column = (z_hi if w == 0 else 1 - z_hi) * 16 + y_at[v] * 4 + x
            scores = jnp.where(lane == column, one, scores)
    scores = scores * (1.0 / (total_width * seq_len))
    for b in range(RING):
        tiles[b] = jnp.where(row == 2 * z_lo + core, jnp.broadcast_to(scores[b : b + 1], (8, 128)), 0.0)
    for b, d, device in group:
        send(("out", b, d), tiles.at[b], arrived.at[b, d], device)
    total = tiles[0]
    for b, d, _ in group:
        got(("out", b, d))
        total = total + arrived[b, d]
    out_ref[...] = total[: out_ref.shape[0], : out_ref.shape[1]]
    for copy in copies.values():
        copy.wait_send()


N_COPIES = 12 + 24 + 6 + 2 + 16 + 15


def per_device(train_act, train_grad, val_act, val_grad):
    n_train, seq_len, width = train_act.shape
    n_val = lax.axis_size("dp")
    bf16, f32 = train_act.dtype, jnp.float32
    anywhere = pl.BlockSpec(memory_space=pl.ANY)
    return pl.pallas_call(
        functools.partial(kernel, width * lax.axis_size("tensor")),
        out_shape=jax.ShapeDtypeStruct((n_train, n_val), f32),
        in_specs=[anywhere] * 4,
        out_specs=pl.BlockSpec(memory_space=pltpu.VMEM),
        scratch_shapes=[
            pltpu.VMEM((2, 2, RING, 2, seq_len, width), bf16),
            pltpu.VMEM((2, 2, RING, 2, seq_len, width), bf16),
            pltpu.VMEM((RING, RING, 2, 2, seq_len, 2 * seq_len), f32),
            pltpu.VMEM((RING, RING, 2, seq_len, 2 * seq_len), f32),
            pltpu.VMEM((8, RING * 2 * seq_len), f32),
            pltpu.VMEM((RING, 8, 128), f32),
            pltpu.VMEM((RING, 4, 8, 128), f32),
            pltpu.SemaphoreType.DMA((4,)),
            pltpu.SemaphoreType.DMA((N_COPIES,)),
            pltpu.SemaphoreType.DMA((N_COPIES,)),
        ],
        compiler_params=pltpu.CompilerParams(
            collective_id=0, has_side_effects=True, vmem_limit_bytes=56 * 1024 * 1024
        ),
        cost_estimate=pl.CostEstimate(
            flops=4 * 64 * (2 * seq_len) ** 2 * width, bytes_accessed=3_300_000, transcendentals=0
        ),
    )(train_act, train_grad, val_act, val_grad)


def solution(mesh):
    placed = P("dp", None, "tensor")
    return jax.shard_map(
        per_device, mesh=mesh, in_specs=(placed,) * 4, out_specs=P("dp", None), check_vma=False
    )
```

```python
import functools

import jax
import jax.numpy as jnp
from jax import lax
from jax.experimental import pallas as pl
from jax.experimental.pallas import tpu as pltpu
from jax.sharding import PartitionSpec as P

MESH = pl.DeviceIdType.MESH
RING = 4


def kernel(
    total_width,
    train_act,
    train_grad,
    val_act,
    val_grad,
    out_ref,
    trains,
    vals,
    grams,
    from_core,
    sums,
    tiles,
    arrived,
    local_sem,
    send_sem,
    recv_sem,
    core_send_sem,
    core_recv_sem,
):
    seq_len = train_act.shape[1]
    train_in = (train_act, train_grad)
    val_in = (val_act, val_grad)

    dp = lax.axis_index("dp")
    tensor = lax.axis_index("tensor")
    z_hi, y, x = dp // 16, (dp // 4) % 4, dp % 4
    z_lo, core = tensor // 2, tensor % 2

    def at(z_hi, y, x, z_lo, core):
        return (z_hi * 16 + y * 4 + x, z_lo * 2 + core)

    x_next, x_prev = (x + 1) % 4, (x + 3) % 4
    y_next, y_prev = (y + 1) % 4, (y + 3) % 4
    to_x_next = at(z_hi, y, x_next, z_lo, core)
    to_x_prev = at(z_hi, y, x_prev, z_lo, core)
    to_y_next = at(z_hi, y_next, x, z_lo, core)
    to_y_prev = at(z_hi, y_prev, x, z_lo, core)
    to_lo = at(z_hi, y, x, 1 - z_lo, core)
    to_hi = at(1 - z_hi, y, x, 1 - z_lo, core)
    to_core = at(z_hi, y, x, z_lo, 1 - core)
    x_at = (x, x_prev, x_next, (x + 2) % 4)
    y_at = (y, y_prev, y_next, (y + 2) % 4)

    mine = pl.ds(z_lo * 2, 2)
    theirs = pl.ds((1 - z_lo) * 2, 2)
    local = []
    for m in range(2):
        local.append(
            pltpu.make_async_copy(train_in[m].at[mine], trains.at[m, 0, 0], local_sem.at[m])
        )
        local.append(
            pltpu.make_async_copy(val_in[m], vals.at[m, 0, 0, pl.ds(0, 1)], local_sem.at[2 + m])
        )
    for copy in local:
        copy.start()

    group = [
        (b, d, at(z_hi, y, x_at[b], *((z_lo, core), (z_lo, 1 - core), (1 - z_lo, core), (1 - z_lo, 1 - core))[d]))
        for b in range(RING)
        for d in range(4)
        if (b, d) != (0, 0)
    ]
    barrier = pltpu.get_barrier_semaphore()
    partners = [to_x_next, to_x_prev, to_y_next, to_y_prev, to_lo, to_hi, to_core]
    for device in partners:
        pl.semaphore_signal(barrier, inc=1, device_id=device, device_id_type=MESH)
    pl.semaphore_wait(barrier, len(partners))

    copies = {}

    def send(name, src, dst, device):
        key = len(copies)
        copies[name] = pltpu.make_async_remote_copy(
            src_ref=src,
            dst_ref=dst,
            send_sem=send_sem.at[key],
            recv_sem=recv_sem.at[key],
            device_id=device,
            device_id_type=MESH,
        )
        copies[name].start()

    def got(name):
        copies[name].wait_recv()

    def x_direct(s, m):
        src = train_in[m].at[mine] if s == 0 else trains.at[m, 1, 0]
        ways = [(1, to_x_next), (2, to_x_prev)]
        for place, device in ways if m == 0 else ways[::-1]:
            send(("x", s, m, place), src, trains.at[m, s, place], device)

    def x_forward(s, m):
        got(("x", s, m, 1 + m))
        send(("x", s, m, 3), trains.at[m, s, 1 + m], trains.at[m, s, 3], (to_x_next, to_x_prev)[m])

    def x_near(s):
        for m in range(2):
            got(("x", s, m, 2 - m))

    def x_far(s):
        for m in range(2):
            got(("x", s, m, 3))

    def y_direct(s, w, m):
        src = val_in[m] if (s, w) == (0, 0) else vals.at[m, s, 0, pl.ds(w, 1)]
        ways = [(1, to_y_next), (2, to_y_prev)]
        for place, device in ways if m == 0 else ways[::-1]:
            send(("y", s, w, m, place), src, vals.at[m, s, place, pl.ds(w, 1)], device)

    def y_forward(s, w, m):
        got(("y", s, w, m, 1 + m))
        here = vals.at[m, s, 1 + m, pl.ds(w, 1)]
        send(("y", s, w, m, 3), here, vals.at[m, s, 3, pl.ds(w, 1)], (to_y_next, to_y_prev)[m])

    def y_near(s, w):
        for m in range(2):
            got(("y", s, w, m, 2 - m))

    def y_far(s, w):
        for m in range(2):
            got(("y", s, w, m, 3))

    def core_copy(b, v):
        return pltpu.make_async_remote_copy(
            src_ref=grams.at[b, v, 1 - core],
            dst_ref=from_core.at[b, v],
            send_sem=core_send_sem.at[b, v],
            recv_sem=core_recv_sem.at[b, v],
            device_id=to_core,
            device_id_type=MESH,
        )

    def gram(s, b, first, last):
        def one(v, carry):
            for m in range(2):
                left = trains[m, s, b].reshape(2 * seq_len, -1)
                right = vals[m, s, v].reshape(2 * seq_len, -1)
                part = lax.dot_general(
                    left, right, (((1,), (1,)), ((), ())), preferred_element_type=jnp.float32
                )
                for r in range(2):
                    rows = part[r * seq_len : (r + 1) * seq_len]
                    if s == 0:
                        grams[b, v, r, m] = rows
                    else:
                        grams[b, v, r, m] += rows
            if s == 1:
                core_copy(b, v).start()
            return carry

        lax.fori_loop(first, last, one, 0)

    def finish(b, first, last):
        def one(v, carry):
            core_copy(b, v).wait_recv()
            act = grams[b, v, core, 0] + from_core[b, v, 0]
            grad = grams[b, v, core, 1] + from_core[b, v, 1]
            sums[v, pl.ds(b, 1)] = jnp.sum(act * grad, axis=0, keepdims=True)
            return carry

        lax.fori_loop(first, last, one, 0)

    sums[...] = jnp.zeros_like(sums)
    for m in range(2):
        x_direct(0, m)
        y_direct(0, 0, m)
        send(("hi", m), val_in[m], vals.at[m, 1, 0, pl.ds(1, 1)], to_hi)
    send(("swap", 0), train_in[0].at[theirs], trains.at[0, 1, 0], to_lo)
    for m in range(2):
        send(("lo", m), val_in[m], vals.at[m, 1, 0, pl.ds(0, 1)], to_lo)
    for copy in local:
        copy.wait()

    for m in range(2):
        y_forward(0, 0, m)
    for m in range(2):
        got(("hi", m))
        y_direct(1, 1, m)
    x_forward(0, 0)
    x_forward(0, 1)
    got(("swap", 0))
    x_direct(1, 0)
    for m in range(2):
        got(("lo", m))
        send(("far", m), vals.at[m, 1, 0, pl.ds(0, 1)], vals.at[m, 0, 0, pl.ds(1, 1)], to_hi)
    send(("swap", 1), train_in[1].at[theirs], trains.at[1, 1, 0], to_lo)
    y_near(0, 0)
    y_far(0, 0)
    for m in range(2):
        y_forward(1, 1, m)
    for m in range(2):
        got(("far", m))
        y_direct(0, 1, m)
    got(("swap", 1))
    x_direct(1, 1)
    x_near(0)
    x_far(0)
    y_near(1, 1)
    y_far(1, 1)
    for m in range(2):
        y_direct(1, 0, m)
    for m in range(2):
        y_forward(0, 1, m)
    x_forward(1, 0)
    y_near(0, 1)
    y_far(0, 1)
    gram(0, 0, 0, RING)
    gram(0, 1, 0, RING)
    x_forward(1, 1)
    for m in range(2):
        y_forward(1, 0, m)
    gram(0, 2, 0, RING)
    gram(0, 3, 0, RING)
    x_near(1)
    y_near(1, 0)
    for b in range(3):
        gram(1, b, 0, 3)
    for b in range(3):
        finish(b, 0, 3)
    y_far(1, 0)
    for b in range(3):
        gram(1, b, 3, RING)
    x_far(1)
    gram(1, 3, 0, RING)
    for b in range(3):
        finish(b, 3, RING)
    finish(3, 0, RING)

    lane = lax.broadcasted_iota(jnp.int32, (8, 128), 1)
    row = lax.broadcasted_iota(jnp.int32, (8, 128), 0)
    scores = jnp.zeros((8, 128), jnp.float32)
    for v in range(RING):
        for w in range(2):
            one = jnp.sum(sums[v, :, w * seq_len : (w + 1) * seq_len], axis=1, keepdims=True)
            column = (z_hi if w == 0 else 1 - z_hi) * 16 + y_at[v] * 4 + x
            scores = jnp.where(lane == column, one, scores)
    scores = scores * (1.0 / (total_width * seq_len))
    for b in range(RING):
        tiles[b] = jnp.where(row == 2 * z_lo + core, jnp.broadcast_to(scores[b : b + 1], (8, 128)), 0.0)
    for b, d, device in group:
        send(("out", b, d), tiles.at[b], arrived.at[b, d], device)
    total = tiles[0]
    for b, d, _ in group:
        got(("out", b, d))
        total = total + arrived[b, d]
    out_ref[...] = total[: out_ref.shape[0], : out_ref.shape[1]]
    for copy in copies.values():
        copy.wait_send()
    for b in range(RING):
        for v in range(RING):
            core_copy(b, v).wait_send()


N_COPIES = 12 + 24 + 6 + 2 + 15


def per_device(train_act, train_grad, val_act, val_grad):
    n_train, seq_len, width = train_act.shape
    n_val = lax.axis_size("dp")
    bf16, f32 = train_act.dtype, jnp.float32
    anywhere = pl.BlockSpec(memory_space=pl.ANY)
    return pl.pallas_call(
        functools.partial(kernel, width * lax.axis_size("tensor")),
        out_shape=jax.ShapeDtypeStruct((n_train, n_val), f32),
        in_specs=[anywhere] * 4,
        out_specs=pl.BlockSpec(memory_space=pltpu.VMEM),
        scratch_shapes=[
            pltpu.VMEM((2, 2, RING, 2, seq_len, width), bf16),
            pltpu.VMEM((2, 2, RING, 2, seq_len, width), bf16),
            pltpu.VMEM((RING, RING, 2, 2, seq_len, 2 * seq_len), f32),
            pltpu.VMEM((RING, RING, 2, seq_len, 2 * seq_len), f32),
            pltpu.VMEM((RING, 8, 2 * seq_len), f32),
            pltpu.VMEM((RING, 8, 128), f32),
            pltpu.VMEM((RING, 4, 8, 128), f32),
            pltpu.SemaphoreType.DMA((4,)),
            pltpu.SemaphoreType.DMA((N_COPIES,)),
            pltpu.SemaphoreType.DMA((N_COPIES,)),
            pltpu.SemaphoreType.DMA((RING, RING)),
            pltpu.SemaphoreType.DMA((RING, RING)),
        ],
        compiler_params=pltpu.CompilerParams(
            collective_id=0, has_side_effects=True, vmem_limit_bytes=56 * 1024 * 1024
        ),
        cost_estimate=pl.CostEstimate(
            flops=4 * 64 * (2 * seq_len) ** 2 * width, bytes_accessed=3_300_000, transcendentals=0
        ),
    )(train_act, train_grad, val_act, val_grad)


def solution(mesh):
    placed = P("dp", None, "tensor")
    return jax.shard_map(
        per_device, mesh=mesh, in_specs=(placed,) * 4, out_specs=P("dp", None), check_vma=False
    )
```

```python
import functools

import jax
import jax.numpy as jnp
from jax import lax
from jax.experimental import pallas as pl
from jax.experimental.pallas import tpu as pltpu
from jax.sharding import PartitionSpec as P

MESH = pl.DeviceIdType.MESH
RING = 4

PLACES = {"n": (0, 1, 2), "f": (3,)}
VALS = {"o": (0,), "n": (1, 2), "f": (3,)}

ORDER = (
    ("hi", 0), ("lo", 0), ("y", 0, 0, 0, 1), ("y", 0, 0, 0, 2), ("hi", 1), ("lo", 1), ("x", 0, 0, 1),
    ("x", 0, 0, 2), ("y", 0, 0, 1, 1), ("y", 0, 0, 1, 2), ("far", 0), ("y", 1, 1, 0, 1), ("y", 1, 1, 0, 2),
    ("gram", 0, 0, "n", "o"), ("far", 1), ("swap", 0), ("x", 0, 1, 1), ("x", 0, 1, 2), ("y", 1, 0, 0, 1),
    ("y", 1, 0, 0, 2), ("gram", 0, 1, "n", "o"), ("y", 0, 0, 0, 3, 1), ("y", 0, 0, 0, 3, 2),
    ("x", 0, 0, 3, 1), ("x", 0, 0, 3, 2), ("gram", 0, 0, "f", "o"), ("y", 1, 1, 1, 1), ("y", 1, 1, 1, 2),
    ("swap", 1), ("y", 1, 0, 1, 1), ("y", 1, 0, 1, 2), ("y", 0, 0, 1, 3, 1), ("y", 0, 0, 1, 3, 2),
    ("x", 1, 0, 1), ("x", 1, 0, 2), ("gram", 1, 0, "n", "o"), ("zs", 1, 1), ("y", 0, 1, 0, 1),
    ("y", 0, 1, 0, 2), ("x", 0, 1, 3, 1), ("x", 0, 1, 3, 2), ("gram", 0, 0, "n", "n"),
    ("gram", 0, 0, "f", "n"), ("gram", 1, 0, "n", "n"), ("y", 1, 1, 0, 3, 1), ("y", 1, 1, 0, 3, 2),
    ("gram", 0, 1, "f", "o"), ("zs", 1, 2), ("gram", 0, 1, "n", "n"), ("y", 1, 0, 0, 3, 1),
    ("y", 1, 0, 0, 3, 2), ("gram", 0, 1, "f", "n"), ("y", 1, 1, 1, 3, 1), ("y", 1, 1, 1, 3, 2),
    ("y", 1, 0, 1, 3, 1), ("y", 1, 0, 1, 3, 2), ("x", 1, 1, 1), ("x", 1, 1, 2), ("gram", 1, 1, "n", "o"),
    ("gram", 1, 1, "n", "n"), ("y", 0, 1, 0, 3, 1), ("y", 0, 1, 0, 3, 2), ("gram", 0, 0, "n", "f"),
    ("gram", 0, 0, "f", "f"), ("gram", 1, 0, "n", "f"), ("x", 1, 0, 3, 1), ("x", 1, 0, 3, 2),
    ("gram", 1, 0, "f", "o"), ("gram", 1, 0, "f", "n"), ("gram", 1, 0, "f", "f"), ("zs", 1, 3),
    ("gram", 0, 1, "n", "f"), ("gram", 0, 1, "f", "f"), ("gram", 1, 1, "n", "f"), ("out", "n"),
    ("x", 1, 1, 3, 1), ("x", 1, 1, 3, 2), ("gram", 1, 1, "f", "o"), ("gram", 1, 1, "f", "n"),
    ("gram", 1, 1, "f", "f"), ("out", "f"),
)


def kernel(
    total_width,
    train_act,
    train_grad,
    val_act,
    val_grad,
    out_ref,
    trains,
    vals,
    grams,
    from_core,
    sums,
    tiles,
    arrived,
    local_sem,
    send_sem,
    recv_sem,
    core_send_sem,
    core_recv_sem,
):
    seq_len = train_act.shape[1]
    train_in = (train_act, train_grad)
    val_in = (val_act, val_grad)

    dp = lax.axis_index("dp")
    tensor = lax.axis_index("tensor")
    z_hi, y, x = dp // 16, (dp // 4) % 4, dp % 4
    z_lo, core = tensor // 2, tensor % 2

    def at(z_hi, y, x, z_lo, core):
        return (z_hi * 16 + y * 4 + x, z_lo * 2 + core)

    x_at = (x, (x + 3) % 4, (x + 1) % 4, (x + 2) % 4)
    y_at = (y, (y + 3) % 4, (y + 1) % 4, (y + 2) % 4)
    to_x = {1: at(z_hi, y, x_at[2], z_lo, core), 2: at(z_hi, y, x_at[1], z_lo, core)}
    to_y = {1: at(z_hi, y_at[2], x, z_lo, core), 2: at(z_hi, y_at[1], x, z_lo, core)}
    to_lo = at(z_hi, y, x, 1 - z_lo, core)
    to_hi = at(1 - z_hi, y, x, 1 - z_lo, core)
    to_core = at(z_hi, y, x, z_lo, 1 - core)

    mine = pl.ds(z_lo * 2, 2)
    theirs = pl.ds((1 - z_lo) * 2, 2)
    local = []
    for m in range(2):
        local.append(
            pltpu.make_async_copy(train_in[m].at[mine], trains.at[m, 0, 0], local_sem.at[m])
        )
        local.append(
            pltpu.make_async_copy(val_in[m], vals.at[m, 0, 0, pl.ds(0, 1)], local_sem.at[2 + m])
        )
    for copy in local:
        copy.start()

    barrier = pltpu.get_barrier_semaphore()
    partners = [to_x[1], to_x[2], to_y[1], to_y[2], to_lo, to_hi, to_core]
    for device in partners:
        pl.semaphore_signal(barrier, inc=1, device_id=device, device_id_type=MESH)
    pl.semaphore_wait(barrier, len(partners))

    copies = {}

    def send(name, src, dst, device):
        key = len(copies)
        copies[name] = pltpu.make_async_remote_copy(
            src_ref=src,
            dst_ref=dst,
            send_sem=send_sem.at[key],
            recv_sem=recv_sem.at[key],
            device_id=device,
            device_id_type=MESH,
        )
        copies[name].start()

    def x_direct(s, m):
        src = train_in[m].at[mine] if s == 0 else trains.at[m, 1, 0]
        for place in (1, 2):
            send(("x", s, m, place), src, trains.at[m, s, place], to_x[place])

    def x_forward(s, m, place):
        half = pl.ds(place - 1, 1)
        send(("x", s, m, 3, place), trains.at[m, s, place, half], trains.at[m, s, 3, half], to_x[place])

    def y_direct(s, w, m):
        if (s, w, m) == (0, 1, 1):
            return
        src = val_in[m] if (s, w) == (0, 0) else vals.at[m, s, 0, pl.ds(w, 1)]
        for place in (1, 2):
            send(("y", s, w, m, place), src, vals.at[m, s, place, pl.ds(w, 1)], to_y[place])

    def y_forward(s, w, m, place):
        half = pl.ds((place - 1) * (seq_len // 2), seq_len // 2)
        send(
            ("y", s, w, m, 3, place),
            vals.at[m, s, place, w, half],
            vals.at[m, s, 3, w, half],
            to_y[place],
        )

    def z_share(m, place):
        send(("zs", m, place), vals.at[m, 1, place, 0], vals.at[m, 0, place, 1], to_hi)

    def core_copy(b, v):
        return pltpu.make_async_remote_copy(
            src_ref=grams.at[0, b, v],
            dst_ref=from_core.at[b, v],
            send_sem=core_send_sem.at[b, v],
            recv_sem=core_recv_sem.at[b, v],
            device_id=to_core,
            device_id_type=MESH,
        )

    def gram(s, m, blocks, val_blocks):
        def one(i, carry):
            b, v = blocks[0] + i // len(val_blocks), val_blocks[0] + i % len(val_blocks)
            part = lax.dot_general(
                trains[m, s, b].reshape(2 * seq_len, -1),
                vals[m, s, v].reshape(2 * seq_len, -1),
                (((1,), (1,)), ((), ())),
                preferred_element_type=jnp.float32,
            )
            if s == 0:
                grams[m, b, v] = part
            elif m == 0:
                grams[0, b, v] += part
                core_copy(b, v).start()
            else:
                core_copy(b, v).wait_recv()
                product = (grams[1, b, v] + part) * (grams[0, b, v] + from_core[b, v])
                sums[v, b] = jnp.sum(product.reshape(2, seq_len, 2 * seq_len), axis=1)
            return carry

        lax.fori_loop(0, len(blocks) * len(val_blocks), one, 0)

    group = ((z_lo, core), (z_lo, 1 - core), (1 - z_lo, core), (1 - z_lo, 1 - core))

    def out(blocks):
        first, last = blocks[0], blocks[-1] + 1
        lane = lax.broadcasted_iota(jnp.int32, (last - first, 2, 128), 2)
        scores = jnp.zeros(lane.shape, jnp.float32)
        for v in range(RING):
            for w in range(2):
                part = sums[v, first:last, :, w * seq_len : (w + 1) * seq_len]
                column = (z_hi if w == 0 else 1 - z_hi) * 16 + y_at[v] * 4 + x
                scores = jnp.where(lane == column, jnp.sum(part, axis=2, keepdims=True), scores)
        scores = scores * (1.0 / (total_width * seq_len))
        row = lax.broadcasted_iota(jnp.int32, (8, 128), 0)
        for b in blocks:
            tile = jnp.zeros((8, 128), jnp.float32)
            for r in range(2):
                tile = jnp.where(row == 2 * z_lo + r, scores[b - first, r : r + 1], tile)
            tiles[b] = tile
            for d, (its_z_lo, its_core) in enumerate(group):
                if (b, d) != (0, 0):
                    device = at(z_hi, y, x_at[b], its_z_lo, its_core)
                    send(("out", b, d), tiles.at[b], arrived.at[b, d], device)

    for m in range(2):
        x_direct(0, m)
        y_direct(0, 0, m)
        send(("hi", m), val_in[m], vals.at[m, 1, 0, pl.ds(1, 1)], to_hi)
        send(("lo", m), val_in[m], vals.at[m, 1, 0, pl.ds(0, 1)], to_lo)
    for m in range(2):
        send(("swap", m), train_in[m].at[theirs], trains.at[m, 1, 0], to_lo)
    for copy in local:
        copy.wait()

    far = set()
    for event in ORDER:
        kind = event[0]
        if kind == "gram":
            gram(event[1], event[2], PLACES[event[3]], VALS[event[4]])
            continue
        if kind == "out":
            out(PLACES[event[1]])
            continue
        copies[event].wait_recv()
        if kind == "hi":
            y_direct(1, 1, event[1])
        elif kind == "lo":
            m = event[1]
            send(("far", m), vals.at[m, 1, 0, pl.ds(0, 1)], vals.at[m, 0, 0, pl.ds(1, 1)], to_hi)
            y_direct(1, 0, m)
        elif kind == "far":
            y_direct(0, 1, event[1])
        elif kind == "swap":
            x_direct(1, event[1])
        elif kind == "x" and event[3] < 3:
            x_forward(*event[1:])
        elif kind == "y":
            s, w, m, place = event[1:5]
            if place < 3:
                y_forward(s, w, m, place)
            shared = (s, w, m) == (1, 0, 1)
            if shared and (place < 3 or event[:5] in far):
                z_share(m, place)
            if place == 3:
                far.add(event[:5])

    total = tiles[0]
    for b in range(RING):
        for d in range(4):
            if (b, d) != (0, 0):
                copies["out", b, d].wait_recv()
                total = total + arrived[b, d]
    out_ref[...] = total[: out_ref.shape[0], : out_ref.shape[1]]
    for copy in copies.values():
        copy.wait_send()
    for b in range(RING):
        for v in range(RING):
            core_copy(b, v).wait_send()


N_COPIES = 4 * 4 + 7 * 4 + (6 + 2 + 3) + 15


def per_device(train_act, train_grad, val_act, val_grad):
    n_train, seq_len, width = train_act.shape
    n_val = lax.axis_size("dp")
    bf16, f32 = train_act.dtype, jnp.float32
    anywhere = pl.BlockSpec(memory_space=pl.ANY)
    return pl.pallas_call(
        functools.partial(kernel, width * lax.axis_size("tensor")),
        out_shape=jax.ShapeDtypeStruct((n_train, n_val), f32),
        in_specs=[anywhere] * 4,
        out_specs=pl.BlockSpec(memory_space=pltpu.VMEM),
        scratch_shapes=[
            pltpu.VMEM((2, 2, RING, 2, seq_len, width), bf16),
            pltpu.VMEM((2, 2, RING, 2, seq_len, width), bf16),
            pltpu.VMEM((2, RING, RING, 2 * seq_len, 2 * seq_len), f32),
            pltpu.VMEM((RING, RING, 2 * seq_len, 2 * seq_len), f32),
            pltpu.VMEM((RING, RING, 2, 2 * seq_len), f32),
            pltpu.VMEM((RING, 8, 128), f32),
            pltpu.VMEM((RING, 4, 8, 128), f32),
            pltpu.SemaphoreType.DMA((4,)),
            pltpu.SemaphoreType.DMA((N_COPIES,)),
            pltpu.SemaphoreType.DMA((N_COPIES,)),
            pltpu.SemaphoreType.DMA((RING, RING)),
            pltpu.SemaphoreType.DMA((RING, RING)),
        ],
        compiler_params=pltpu.CompilerParams(
            collective_id=0, has_side_effects=True, vmem_limit_bytes=56 * 1024 * 1024
        ),
        cost_estimate=pl.CostEstimate(
            flops=4 * 64 * (2 * seq_len) ** 2 * width, bytes_accessed=3_300_000, transcendentals=0
        ),
    )(train_act, train_grad, val_act, val_grad)


def solution(mesh):
    placed = P("dp", None, "tensor")
    return jax.shard_map(
        per_device, mesh=mesh, in_specs=(placed,) * 4, out_specs=P("dp", None), check_vma=False
    )
```

```python
import functools

import jax
import jax.numpy as jnp
from jax import lax
from jax.experimental import pallas as pl
from jax.experimental.pallas import tpu as pltpu
from jax.sharding import PartitionSpec as P

MESH = pl.DeviceIdType.MESH
RING = 4

BLOCKS = {"o": (0, 1), "p": (2, 3)}
PLACES = {"a": (0,), "b": (1, 2), "c": (3,), "d": (4,), "e": (5, 6), "f": (7,)}

ORDER = (
    ("s1", "o", "a", 0), ("s2", "o", "a", 0), ("ra", 0), ("rb", 0), ("y", 0, 0, 0, 1), ("y", 0, 0, 0, 2),
    ("v", 0, 0, 0), ("ra", 1), ("rb", 1), ("s1", "o", "b", 0), ("s3", "o", "a", 0), ("s1", "o", "d", 0),
    ("s2", "o", "b", 0), ("fa", 0), ("s2", "o", "d", 0), ("fb", 0), ("s1", "o", "a", 1), ("x", 0, 0),
    ("y", 0, 0, 1, 1), ("y", 0, 0, 1, 2), ("v", 0, 1, 0), ("fa", 1), ("s2", "o", "a", 1), ("fb", 1),
    ("y", 0, 0, 0, 3, 1), ("y", 0, 0, 0, 3, 2), ("s1", "o", "c", 0), ("s3", "o", "b", 0), ("s3", "o", "d", 0),
    ("s2", "o", "c", 0), ("v", 0, 0, 1), ("s3", "o", "a", 1), ("s4", "o", "a"), ("s3", "o", "c", 0),
    ("y", 0, 1, 0, 1), ("y", 0, 1, 0, 2), ("s1", "o", "b", 1), ("s2", "o", "b", 1), ("x", 0, 1),
    ("v", 0, 0, 2), ("y", 0, 0, 1, 3, 1), ("y", 0, 0, 1, 3, 2), ("s1", "p", "a", 0), ("s1", "p", "b", 0),
    ("s1", "p", "c", 0), ("s1", "p", "d", 0), ("s1", "o", "e", 0), ("s2", "p", "a", 0), ("s2", "p", "b", 0),
    ("s2", "p", "c", 0), ("s1", "p", "e", 0), ("s2", "p", "d", 0), ("s2", "o", "e", 0), ("s3", "o", "b", 1),
    ("s1", "p", "a", 1), ("s1", "p", "b", 1), ("v", 1, 0, 0), ("y", 0, 1, 1, 1), ("y", 0, 1, 1, 2),
    ("s2", "p", "e", 0), ("s3", "p", "a", 0), ("s2", "p", "a", 1), ("s1", "o", "d", 1), ("s2", "p", "b", 1),
    ("s1", "p", "d", 1), ("s3", "p", "b", 0), ("y", 0, 1, 0, 3, 1), ("y", 0, 1, 0, 3, 2), ("s1", "o", "c", 1),
    ("s2", "o", "d", 1), ("s3", "p", "c", 0), ("s1", "p", "c", 1), ("s2", "p", "d", 1), ("s4", "o", "b"),
    ("x", 1, 0), ("v", 0, 1, 1), ("s2", "o", "c", 1), ("s2", "p", "c", 1), ("s3", "p", "d", 0),
    ("s3", "o", "e", 0), ("y", 1, 1, 0, 1), ("y", 1, 1, 0, 2), ("s1", "o", "e", 1), ("s1", "p", "e", 1),
    ("s3", "p", "e", 0), ("s3", "p", "a", 1), ("s2", "o", "e", 1), ("y", 0, 1, 1, 3, 1), ("y", 0, 1, 1, 3, 2),
    ("v", 0, 1, 2), ("s2", "p", "e", 1), ("s3", "p", "b", 1), ("y", 1, 1, 0, 3, 1), ("y", 1, 1, 0, 3, 2),
    ("s3", "o", "d", 1), ("s1", "o", "f", 1), ("s1", "p", "f", 1), ("s3", "p", "d", 1), ("s2", "o", "f", 1),
    ("s2", "p", "f", 1), ("s3", "o", "c", 1), ("x", 1, 1), ("v", 1, 1, 0), ("s4", "p", "a"),
    ("s3", "p", "c", 1), ("s4", "p", "b"), ("s4", "o", "c"), ("s3", "o", "e", 1), ("s4", "p", "c"),
    ("s4", "o", "d"), ("s4", "p", "d"), ("v", 0, 0, 3), ("s3", "p", "e", 1), ("s1", "o", "f", 0),
    ("s1", "p", "f", 0), ("s3", "o", "f", 1), ("y", 1, 1, 1, 1), ("y", 1, 1, 1, 2), ("s4", "o", "e"),
    ("s2", "o", "f", 0), ("s2", "p", "f", 0), ("s3", "p", "f", 1), ("s4", "p", "e"), ("v", 0, 1, 3),
    ("y", 1, 1, 1, 3, 1), ("y", 1, 1, 1, 3, 2), ("s3", "o", "f", 0), ("s3", "p", "f", 0), ("s4", "o", "f"),
    ("s4", "p", "f"),
)

POWER = 16
PEAK = 222.0


def kernel(
    total_width,
    train_act,
    train_grad,
    val_act,
    val_grad,
    out_ref,
    trains,
    vals,
    relay,
    acts,
    from_core,
    coded_out,
    coded_in,
    whole,
    sums,
    tiles,
    arrived,
    local_sem,
    send_sem,
    recv_sem,
):
    seq_len = train_act.shape[1]
    train_in = (train_act, train_grad)
    val_in = (val_act, val_grad)

    dp = lax.axis_index("dp")
    tensor = lax.axis_index("tensor")
    z_hi, y, x = dp // 16, (dp // 4) % 4, dp % 4
    z_lo, core = tensor // 2, tensor % 2

    def at(z_hi, y, x, z_lo, core):
        return (z_hi * 16 + y * 4 + x, z_lo * 2 + core)

    mate, twin = x + 1 - 2 * (x % 2), 3 - x
    y_at = (y, (y + 3) % 4, (y + 1) % 4, (y + 2) % 4)
    to_y = {1: at(z_hi, y_at[2], x, z_lo, core), 2: at(z_hi, y_at[1], x, z_lo, core)}
    to_mate = at(z_hi, y, mate, z_lo, core)
    to_twin = at(z_hi, y, twin, z_lo, core)
    to_lo = at(z_hi, y, x, 1 - z_lo, core)
    to_hi = at(1 - z_hi, y, x, 1 - z_lo, core)
    to_core = at(z_hi, y, x, z_lo, 1 - core)

    local = []
    for m in range(2):
        local.append(
            pltpu.make_async_copy(train_in[m], trains.at[m, pl.ds(0, 4)], local_sem.at[m])
        )
        local.append(
            pltpu.make_async_copy(val_in[m], vals.at[m, 0, pl.ds(0, 1)], local_sem.at[2 + m])
        )
    for copy in local:
        copy.start()

    barrier = pltpu.get_barrier_semaphore()
    partners = [to_mate, to_twin, to_y[1], to_y[2], to_lo, to_hi, to_core]
    for device in partners:
        pl.semaphore_signal(barrier, inc=1, device_id=device, device_id_type=MESH)
    pl.semaphore_wait(barrier, len(partners))

    copies = {}

    def send(name, src, dst, device):
        key = len(copies)
        copies[name] = pltpu.make_async_remote_copy(
            src_ref=src,
            dst_ref=dst,
            send_sem=send_sem.at[key],
            recv_sem=recv_sem.at[key],
            device_id=device,
            device_id_type=MESH,
        )
        copies[name].start()

    def got(name):
        copies[name].wait_recv()

    def own_val(w, m):
        return val_in[m].at[0] if w == 0 else vals.at[m, 0, 1]

    def y_direct(q, w, m):
        src = own_val(w, m) if q == 0 else vals.at[m, RING, w]
        for place in (1, 2):
            send(("y", q, w, m, place), src, vals.at[m, q * RING + place, w], to_y[place])

    def y_forward(q, w, m, place):
        half = pl.ds((place - 1) * (seq_len // 2), seq_len // 2)
        send(
            ("y", q, w, m, 3, place),
            vals.at[m, q * RING + place, w, half],
            vals.at[m, q * RING + 3, w, half],
            to_y[place],
        )

    def v_direct(w, m, place):
        src = own_val(w, m) if place == 0 else vals.at[m, place, w]
        send(("v", w, m, place), src, vals.at[m, RING + place, w], to_twin)

    def own_ready(w, m):
        y_direct(0, w, m)
        v_direct(w, m, 0)

    def have(q, w, m, place):
        if q == 0 and w == 0 and place > 0:
            v_direct(w, m, place)
        if q == 1 and w == 1 and place == 0:
            y_direct(1, w, m)

    starts, rows = {}, {}
    for event in ORDER:
        if event[0] == "s1":
            size = len(BLOCKS[event[1]]) * len(PLACES[event[2]])
            first = sum(n for _, n in starts.values())
            rows[event[1:]] = (first * seq_len + 16 * len(starts), size * seq_len + 16)
            starts[event[1:]] = (first, size)

    def act_product(group):
        blocks, places, w = BLOCKS[group[0]], PLACES[group[1]], group[2]
        first, size = starts[group]
        n = len(blocks)

        def one(i, carry):
            part = lax.dot_general(
                trains[0, 2 * blocks[0] : 2 * blocks[0] + 2 * n].reshape(2 * n * seq_len, -1),
                vals[0, places[0] + i, w],
                (((1,), (1,)), ((), ())),
                preferred_element_type=jnp.float32,
            )
            for k in range(n):
                for r in range(2):
                    at_row = (2 * k + r) * seq_len
                    acts[r, first + i * n + k] = part[at_row : at_row + seq_len]
            return carry

        lax.fori_loop(0, len(places), one, 0)
        send(("s1",) + group, acts.at[1 - core, pl.ds(first, size)], from_core.at[pl.ds(first, size)], to_core)

    def act_cores(group):
        first, size = starts[group]
        row, n_rows = rows[group]
        got(("s1",) + group)

        def add(i, peak):
            value = acts[core, first + i] + from_core[first + i]
            acts[core, first + i] = value
            return jnp.maximum(peak, jnp.max(jnp.abs(value).reshape(seq_len // 8, 8, seq_len), axis=0))

        peak = lax.fori_loop(0, size, add, jnp.zeros((8, seq_len), jnp.float32))
        peak = jnp.max(jnp.max(peak, axis=0, keepdims=True), axis=1, keepdims=True)
        scale = jnp.broadcast_to(jnp.maximum(peak, 1e-30) * 1.01, (16, seq_len)).astype(jnp.bfloat16)
        coded_out[pl.ds(row + size * seq_len, 16)] = scale
        inverse = PEAK / scale.astype(jnp.float32)[0:1]

        def code(i, carry):
            value = acts[core, first + i]
            power = jnp.abs(value) * inverse
            for _ in range(4):
                power = power * power
            power = jnp.where(value < 0, -power, power).astype(jnp.bfloat16)
            coded_out[pl.ds(pl.multiple_of(row + i * seq_len, 16), seq_len)] = power
            return carry

        lax.fori_loop(0, size, code, 0)
        send(("s2",) + group, coded_out.at[pl.ds(row, n_rows)], coded_in.at[pl.ds(row, n_rows)], to_lo)

    def act_whole(group):
        first, size = starts[group]
        row, _ = rows[group]
        got(("s2",) + group)
        scale = coded_in[pl.ds(row + size * seq_len, 16)].astype(jnp.float32)[0:1] * (1.0 / PEAK)

        def one(i, carry):
            power = coded_in[pl.ds(pl.multiple_of(row + i * seq_len, 16), seq_len)].astype(jnp.float32)
            size_of = jnp.abs(power)
            value = jnp.exp(jnp.log(size_of) * (1.0 / POWER)) * scale
            value = jnp.where(power < 0, -value, value)
            whole[core, first + i] = acts[core, first + i] + jnp.where(size_of > 0, value, 0.0)
            return carry

        lax.fori_loop(0, size, one, 0)
        here = whole.at[core, pl.ds(first, size)]
        send(("s3",) + group, here, here, to_core)

    def grad_product(b_key, p_key):
        blocks, places = BLOCKS[b_key], PLACES[p_key]
        n = len(blocks)
        for w in range(2):
            got(("s3", b_key, p_key, w))

        def one(i, carry):
            v, b = places[0] + i // n, blocks[0] + i % n
            part = lax.dot_general(
                trains[1, pl.ds(2 * b, 2)].reshape(2 * seq_len, -1),
                vals[1, v].reshape(2 * seq_len, -1),
                (((1,), (1,)), ((), ())),
                preferred_element_type=jnp.float32,
            )
            for r in range(2):
                for w in range(2):
                    act = whole[r, starts[b_key, p_key, w][0] + i]
                    grad = part[r * seq_len : (r + 1) * seq_len, w * seq_len : (w + 1) * seq_len]
                    sums[v, w, b, r : r + 1] = jnp.sum(act * grad, axis=0, keepdims=True)
            return carry

        lax.fori_loop(0, n * len(places), one, 0)

    group_of = ((z_lo, core), (z_lo, 1 - core), (1 - z_lo, core), (1 - z_lo, 1 - core))

    def out():
        lane = lax.broadcasted_iota(jnp.int32, (RING, 2, 128), 2)
        scores = jnp.zeros(lane.shape, jnp.float32)
        for v in range(2 * RING):
            for w in range(2):
                its_z_hi = z_hi if w == 0 else 1 - z_hi
                column = its_z_hi * 16 + y_at[v % RING] * 4 + (x if v < RING else twin)
                scores = jnp.where(lane == column, jnp.sum(sums[v, w], axis=2, keepdims=True), scores)
        scores = scores * (1.0 / (total_width * seq_len))
        tiles[...] = jnp.zeros_like(tiles)
        for b in range(RING):
            for r in range(2):
                at_row = (b % 2) * 2 + r
                tiles[b // 2, at_row : at_row + 1] = scores[b, r : r + 1]
        for side, its_x in ((1, mate), (0, x)):
            for d, (its_z_lo, its_core) in enumerate(group_of):
                if (side, d) != (0, 0):
                    device = at(z_hi, y, its_x, its_z_lo, its_core)
                    send(("out", side, d), tiles.at[side], arrived.at[side, d], device)

    half_a, half_b = pl.ds(0, seq_len // 2), pl.ds(seq_len // 2, seq_len // 2)
    for m in range(2):
        send(("ra", m), val_in[m].at[0, half_a], relay.at[0, m], to_lo)
        send(("rb", m), val_in[m].at[0, half_b], relay.at[1, m], to_hi)
        for h in range(2):
            send(("x", m, h), train_in[m].at[pl.ds(2 * h, 2)], trains.at[m, pl.ds(4 + 2 * h, 2)], to_mate)
        own_ready(0, m)
    for copy in local:
        copy.wait()

    seen = set()
    for event in ORDER:
        kind = event[0]
        if kind == "s1":
            act_product(event[1:])
            continue
        if kind == "s2":
            act_cores(event[1:])
            continue
        if kind == "s3":
            act_whole(event[1:])
            continue
        if kind == "s4":
            grad_product(*event[1:])
            continue
        got(event)
        if kind == "ra":
            m = event[1]
            send(("fa", m), relay.at[0, m], vals.at[m, 0, 1, half_a], to_hi)
        elif kind == "rb":
            m = event[1]
            send(("fb", m), relay.at[1, m], vals.at[m, 0, 1, half_b], to_lo)
        elif kind in ("fa", "fb"):
            m = event[1]
            if ("f", m) in seen:
                own_ready(1, m)
            seen.add(("f", m))
        elif kind == "v":
            have(1, *event[1:])
        elif kind == "y":
            q, w, m, place = event[1:5]
            if place < 3:
                y_forward(q, w, m, place)
                have(q, w, m, place)
            elif event[:5] in seen:
                have(q, w, m, place)
            seen.add(event[:5])
    out()

    total = tiles[0]
    for side in range(2):
        for d in range(4):
            if (side, d) != (0, 0):
                got(("out", side, d))
                total = total + arrived[side, d]
    out_ref[...] = total[: out_ref.shape[0], : out_ref.shape[1]]
    for copy in copies.values():
        copy.wait_send()


GROUPS = 2 * len(BLOCKS) * len(PLACES)
UNITS = 2 * 4 * 2 * RING
N_COPIES = 8 + 4 + 2 * 3 * 4 + 2 * (RING + 1) + 3 * GROUPS + 7


def per_device(train_act, train_grad, val_act, val_grad):
    n_train, seq_len, width = train_act.shape
    n_val = lax.axis_size("dp")
    bf16, f32 = train_act.dtype, jnp.float32
    anywhere = pl.BlockSpec(memory_space=pl.ANY)
    coded = (UNITS * seq_len + 16 * GROUPS, seq_len)
    return pl.pallas_call(
        functools.partial(kernel, width * lax.axis_size("tensor")),
        out_shape=jax.ShapeDtypeStruct((n_train, n_val), f32),
        in_specs=[anywhere] * 4,
        out_specs=pl.BlockSpec(memory_space=pltpu.VMEM),
        scratch_shapes=[
            pltpu.VMEM((2, 2 * n_train, seq_len, width), bf16),
            pltpu.VMEM((2, 2 * RING, 2, seq_len, width), bf16),
            pltpu.VMEM((2, 2, seq_len // 2, width), bf16),
            pltpu.VMEM((2, UNITS, seq_len, seq_len), f32),
            pltpu.VMEM((UNITS, seq_len, seq_len), f32),
            pltpu.VMEM(coded, bf16),
            pltpu.VMEM(coded, bf16),
            pltpu.VMEM((2, UNITS, seq_len, seq_len), f32),
            pltpu.VMEM((2 * RING, 2, RING, 2, seq_len), f32),
            pltpu.VMEM((2, 8, 128), f32),
            pltpu.VMEM((2, 4, 8, 128), f32),
            pltpu.SemaphoreType.DMA((4,)),
            pltpu.SemaphoreType.DMA((N_COPIES,)),
            pltpu.SemaphoreType.DMA((N_COPIES,)),
        ],
        compiler_params=pltpu.CompilerParams(
            collective_id=0, has_side_effects=True, vmem_limit_bytes=56 * 1024 * 1024
        ),
        cost_estimate=pl.CostEstimate(
            flops=4 * 32 * (2 * seq_len) ** 2 * width, bytes_accessed=3_300_000, transcendentals=0
        ),
    )(train_act, train_grad, val_act, val_grad)


def solution(mesh):
    placed = P("dp", None, "tensor")
    return jax.shard_map(
        per_device, mesh=mesh, in_specs=(placed,) * 4, out_specs=P("dp", None), check_vma=False
    )
```

```python
import functools

import jax
import jax.numpy as jnp
from jax import lax
from jax.experimental import pallas as pl
from jax.experimental.pallas import tpu as pltpu
from jax.sharding import PartitionSpec as P

MESH = pl.DeviceIdType.MESH
RING = 4

BLOCKS = {"o": (0, 1), "p": (2,), "s": (3,)}
PLACES = {"a": (0,), "b": (1, 2), "c": (3,), "d": (4,), "e": (5, 6), "f": (7,)}

PIECES = (
    (0, 0, 0, 32, "v"),
    (0, 0, 32, 96, "y"),
    (1, 0, 0, 128, "v"),
    (0, 1, 0, 128, "y"),
    (1, 1, 0, 128, "v"),
)

ORDER = (
    ("s1", "o", "a", 0), ("s2", "o", "a", 0), ("v", 0, 0), ("y", 0, 0, 1), ("y", 0, 0, 2), ("ra", 0),
    ("rb", 0), ("v", 1, 0), ("y", 0, 1, 1), ("y", 0, 1, 2), ("ra", 1), ("rb", 1), ("s1", "o", "b", 0),
    ("s3", "o", "a", 0), ("s1", "o", "d", 0), ("s2", "o", "b", 0), ("fa", 0), ("s2", "o", "d", 0), ("fb", 0),
    ("s1", "o", "a", 1), ("v", 3, 0), ("y", 0, 3, 1), ("y", 0, 3, 2), ("x", 0, 0), ("fa", 1),
    ("s2", "o", "a", 1), ("s1", "p", "a", 0), ("s1", "p", "b", 0), ("fb", 1), ("s1", "p", "d", 0),
    ("y", 1, 0, 1), ("y", 1, 0, 2), ("s1", "p", "a", 1), ("y", 0, 0, 3, 1), ("y", 0, 0, 3, 2),
    ("s2", "p", "a", 0), ("s2", "p", "b", 0), ("s2", "p", "d", 0), ("s2", "p", "a", 1), ("s3", "o", "b", 0),
    ("y", 0, 1, 3, 1), ("v", 1, 1), ("y", 0, 1, 3, 2), ("s1", "o", "c", 0), ("s3", "o", "d", 0),
    ("s1", "p", "c", 0), ("s3", "o", "a", 1), ("s2", "o", "c", 0), ("s3", "p", "a", 0), ("s2", "p", "c", 0),
    ("s4", "o", "a"), ("s3", "p", "b", 0), ("v", 1, 2), ("s3", "p", "d", 0), ("s1", "o", "e", 0),
    ("s3", "p", "a", 1), ("s1", "p", "e", 0), ("y", 0, 2, 1), ("y", 0, 2, 2), ("s1", "o", "b", 1),
    ("s3", "o", "c", 0), ("s2", "o", "e", 0), ("x", 0, 1), ("s2", "p", "e", 0), ("s3", "p", "c", 0),
    ("s1", "s", "a", 0), ("s1", "s", "b", 0), ("s2", "o", "b", 1), ("s1", "s", "c", 0), ("y", 0, 3, 3, 1),
    ("y", 0, 3, 3, 2), ("s1", "s", "d", 0), ("s1", "s", "e", 0), ("s2", "s", "a", 0), ("s1", "s", "a", 1),
    ("s2", "s", "b", 0), ("s1", "p", "b", 1), ("v", 2, 0), ("s2", "s", "c", 0), ("s1", "s", "b", 1),
    ("s2", "s", "d", 0), ("s1", "o", "d", 1), ("s2", "s", "e", 0), ("s2", "s", "a", 1), ("s3", "o", "e", 0),
    ("s2", "p", "b", 1), ("s1", "p", "d", 1), ("s2", "s", "b", 1), ("s3", "p", "e", 0), ("s2", "o", "d", 1),
    ("s1", "s", "d", 1), ("s2", "p", "d", 1), ("y", 0, 4, 1), ("y", 0, 4, 2), ("s2", "s", "d", 1),
    ("s3", "o", "b", 1), ("y", 1, 0, 3, 1), ("y", 1, 0, 3, 2), ("s3", "s", "a", 0), ("v", 3, 1),
    ("s3", "s", "b", 0), ("s4", "o", "b"), ("y", 0, 2, 3, 1), ("y", 0, 2, 3, 2), ("s3", "s", "c", 0),
    ("x", 1, 0), ("s3", "s", "d", 0), ("s1", "o", "c", 1), ("s3", "s", "e", 0), ("s1", "p", "c", 1),
    ("s1", "s", "c", 1), ("s4", "p", "a"), ("s3", "s", "a", 1), ("s2", "o", "c", 1), ("s3", "p", "b", 1),
    ("s2", "p", "c", 1), ("s2", "s", "c", 1), ("v", 3, 2), ("s3", "s", "b", 1), ("s4", "p", "b"),
    ("s3", "o", "d", 1), ("y", 1, 2, 1), ("y", 1, 2, 2), ("s1", "o", "e", 1), ("s3", "p", "d", 1),
    ("s1", "p", "e", 1), ("s3", "s", "d", 1), ("s1", "s", "e", 1), ("s3", "o", "c", 1), ("s2", "o", "e", 1),
    ("y", 0, 4, 3, 1), ("y", 0, 4, 3, 2), ("s2", "p", "e", 1), ("s2", "s", "e", 1), ("s3", "p", "c", 1),
    ("v", 4, 0), ("s3", "s", "c", 1), ("s4", "o", "d"), ("s4", "o", "c"), ("s4", "p", "c"), ("y", 1, 2, 3, 1),
    ("y", 1, 2, 3, 2), ("s1", "o", "f", 1), ("s1", "p", "f", 1), ("x", 1, 1), ("s1", "s", "f", 1),
    ("s4", "p", "d"), ("s3", "o", "e", 1), ("s4", "s", "a"), ("v", 1, 3), ("s2", "o", "f", 1),
    ("s2", "p", "f", 1), ("s2", "s", "f", 1), ("s3", "p", "e", 1), ("s1", "o", "f", 0), ("s1", "p", "f", 0),
    ("s1", "s", "f", 0), ("s4", "s", "b"), ("s3", "s", "e", 1), ("s4", "s", "c"), ("s2", "o", "f", 0),
    ("s2", "p", "f", 0), ("s2", "s", "f", 0), ("s4", "s", "d"), ("s3", "o", "f", 1), ("y", 1, 4, 1),
    ("y", 1, 4, 2), ("s3", "p", "f", 1), ("s4", "o", "e"), ("s3", "s", "f", 1), ("s4", "p", "e"), ("v", 3, 3),
    ("s3", "o", "f", 0), ("s3", "p", "f", 0), ("s4", "s", "e"), ("s3", "s", "f", 0), ("y", 1, 4, 3, 1),
    ("y", 1, 4, 3, 2), ("s4", "o", "f"), ("s4", "p", "f"), ("s4", "s", "f"),
)

POWER = 16
PEAK = 222.0


def kernel(
    total_width,
    train_act,
    train_grad,
    val_act,
    val_grad,
    out_ref,
    trains,
    vals,
    relay,
    acts,
    from_core,
    coded_out,
    coded_in,
    whole,
    sums,
    tiles,
    arrived,
    local_sem,
    send_sem,
    recv_sem,
):
    seq_len = train_act.shape[1]
    train_in = (train_act, train_grad)
    val_in = (val_act, val_grad)

    dp = lax.axis_index("dp")
    tensor = lax.axis_index("tensor")
    z_hi, y, x = dp // 16, (dp // 4) % 4, dp % 4
    z_lo, core = tensor // 2, tensor % 2

    def at(z_hi, y, x, z_lo, core):
        return (z_hi * 16 + y * 4 + x, z_lo * 2 + core)

    mate, twin = x + 1 - 2 * (x % 2), 3 - x
    y_at = (y, (y + 3) % 4, (y + 1) % 4, (y + 2) % 4)
    to_y = {1: at(z_hi, y_at[2], x, z_lo, core), 2: at(z_hi, y_at[1], x, z_lo, core)}
    to_mate = at(z_hi, y, mate, z_lo, core)
    to_twin = at(z_hi, y, twin, z_lo, core)
    to_lo = at(z_hi, y, x, 1 - z_lo, core)
    to_hi = at(1 - z_hi, y, x, 1 - z_lo, core)
    to_core = at(z_hi, y, x, z_lo, 1 - core)

    local = []
    for m in range(2):
        local.append(
            pltpu.make_async_copy(train_in[m], trains.at[m, pl.ds(0, 4)], local_sem.at[m])
        )
        local.append(
            pltpu.make_async_copy(val_in[m], vals.at[m, 0, pl.ds(0, 1)], local_sem.at[2 + m])
        )
    for copy in local:
        copy.start()

    barrier = pltpu.get_barrier_semaphore()
    partners = [to_mate, to_twin, to_y[1], to_y[2], to_lo, to_hi, to_core]
    for device in partners:
        pl.semaphore_signal(barrier, inc=1, device_id=device, device_id_type=MESH)
    pl.semaphore_wait(barrier, len(partners))

    copies = {}

    def send(name, src, dst, device):
        key = len(copies)
        copies[name] = pltpu.make_async_remote_copy(
            src_ref=src,
            dst_ref=dst,
            send_sem=send_sem.at[key],
            recv_sem=recv_sem.at[key],
            device_id=device,
            device_id_type=MESH,
        )
        copies[name].start()

    def got(name):
        copies[name].wait_recv()

    def own_val(piece):
        w, m, row, rows, _ = PIECES[piece]
        rows = pl.ds(row, rows)
        return val_in[m].at[0, rows] if w == 0 else vals.at[m, 0, 1, rows]

    def y_direct(q, piece):
        w, m, row, rows, _ = PIECES[piece]
        src = own_val(piece) if q == 0 else vals.at[m, RING, w, pl.ds(row, rows)]
        for place in (1, 2):
            dst = vals.at[m, q * RING + place, w, pl.ds(row, rows)]
            send(("y", q, piece, place), src, dst, to_y[place])

    def y_forward(q, piece, place):
        w, m, row, rows, _ = PIECES[piece]
        half = pl.ds(row + (place - 1) * (rows // 2), rows // 2)
        send(
            ("y", q, piece, 3, place),
            vals.at[m, q * RING + place, w, half],
            vals.at[m, q * RING + 3, w, half],
            to_y[place],
        )

    def v_direct(piece, place):
        w, m, row, rows, _ = PIECES[piece]
        src = own_val(piece) if place == 0 else vals.at[m, place, w, pl.ds(row, rows)]
        send(("v", piece, place), src, vals.at[m, RING + place, w, pl.ds(row, rows)], to_twin)

    def own_ready(w, m):
        for piece, what in enumerate(PIECES):
            if what[:2] == (w, m):
                v_direct(piece, 0)
                y_direct(0, piece)

    def have(q, piece, place):
        first = PIECES[piece][4]
        if first == "y" and q == 0 and place > 0:
            v_direct(piece, place)
        if first == "v" and q == 1 and place == 0:
            y_direct(1, piece)

    starts, rows = {}, {}
    for event in ORDER:
        if event[0] == "s1":
            size = len(BLOCKS[event[1]]) * len(PLACES[event[2]])
            first = sum(n for _, n in starts.values())
            rows[event[1:]] = (first * seq_len + 16 * len(starts), size * seq_len + 16)
            starts[event[1:]] = (first, size)

    def act_product(group):
        blocks, places, w = BLOCKS[group[0]], PLACES[group[1]], group[2]
        first, size = starts[group]
        n = len(blocks)

        def one(i, carry):
            part = lax.dot_general(
                trains[0, 2 * blocks[0] : 2 * blocks[0] + 2 * n].reshape(2 * n * seq_len, -1),
                vals[0, places[0] + i, w],
                (((1,), (1,)), ((), ())),
                preferred_element_type=jnp.float32,
            )
            for k in range(n):
                for r in range(2):
                    at_row = (2 * k + r) * seq_len
                    acts[r, first + i * n + k] = part[at_row : at_row + seq_len]
            return carry

        lax.fori_loop(0, len(places), one, 0)
        send(("s1",) + group, acts.at[1 - core, pl.ds(first, size)], from_core.at[pl.ds(first, size)], to_core)

    def act_cores(group):
        first, size = starts[group]
        row, n_rows = rows[group]
        got(("s1",) + group)

        def add(i, peak):
            value = acts[core, first + i] + from_core[first + i]
            acts[core, first + i] = value
            return jnp.maximum(peak, jnp.max(jnp.abs(value).reshape(seq_len // 8, 8, seq_len), axis=0))

        peak = lax.fori_loop(0, size, add, jnp.zeros((8, seq_len), jnp.float32))
        peak = jnp.max(jnp.max(peak, axis=0, keepdims=True), axis=1, keepdims=True)
        scale = jnp.broadcast_to(jnp.maximum(peak, 1e-30) * 1.01, (16, seq_len)).astype(jnp.bfloat16)
        coded_out[pl.ds(row + size * seq_len, 16)] = scale
        inverse = PEAK / scale.astype(jnp.float32)[0:1]

        def code(i, carry):
            value = acts[core, first + i]
            power = jnp.abs(value) * inverse
            for _ in range(4):
                power = power * power
            power = jnp.where(value < 0, -power, power).astype(jnp.bfloat16)
            coded_out[pl.ds(pl.multiple_of(row + i * seq_len, 16), seq_len)] = power
            return carry

        lax.fori_loop(0, size, code, 0)
        send(("s2",) + group, coded_out.at[pl.ds(row, n_rows)], coded_in.at[pl.ds(row, n_rows)], to_lo)

    def act_whole(group):
        first, size = starts[group]
        row, _ = rows[group]
        got(("s2",) + group)
        scale = coded_in[pl.ds(row + size * seq_len, 16)].astype(jnp.float32)[0:1] * (1.0 / PEAK)

        def one(i, carry):
            power = coded_in[pl.ds(pl.multiple_of(row + i * seq_len, 16), seq_len)].astype(jnp.float32)
            size_of = jnp.abs(power)
            value = jnp.exp(jnp.log(size_of) * (1.0 / POWER)) * scale
            value = jnp.where(power < 0, -value, value)
            whole[core, first + i] = acts[core, first + i] + jnp.where(size_of > 0, value, 0.0)
            return carry

        lax.fori_loop(0, size, one, 0)
        here = whole.at[core, pl.ds(first, size)]
        send(("s3",) + group, here, here, to_core)

    def grad_product(b_key, p_key):
        blocks, places = BLOCKS[b_key], PLACES[p_key]
        n = len(blocks)
        for w in range(2):
            got(("s3", b_key, p_key, w))

        def one(i, carry):
            v, b = places[0] + i // n, blocks[0] + i % n
            part = lax.dot_general(
                trains[1, pl.ds(2 * b, 2)].reshape(2 * seq_len, -1),
                vals[1, v].reshape(2 * seq_len, -1),
                (((1,), (1,)), ((), ())),
                preferred_element_type=jnp.float32,
            )
            for r in range(2):
                for w in range(2):
                    act = whole[r, starts[b_key, p_key, w][0] + i]
                    grad = part[r * seq_len : (r + 1) * seq_len, w * seq_len : (w + 1) * seq_len]
                    sums[v, w, b, r : r + 1] = jnp.sum(act * grad, axis=0, keepdims=True)
            return carry

        lax.fori_loop(0, n * len(places), one, 0)

    group_of = ((z_lo, core), (z_lo, 1 - core), (1 - z_lo, core), (1 - z_lo, 1 - core))

    def out():
        lane = lax.broadcasted_iota(jnp.int32, (RING, 2, 128), 2)
        scores = jnp.zeros(lane.shape, jnp.float32)
        for v in range(2 * RING):
            for w in range(2):
                its_z_hi = z_hi if w == 0 else 1 - z_hi
                column = its_z_hi * 16 + y_at[v % RING] * 4 + (x if v < RING else twin)
                scores = jnp.where(lane == column, jnp.sum(sums[v, w], axis=2, keepdims=True), scores)
        scores = scores * (1.0 / (total_width * seq_len))
        tiles[...] = jnp.zeros_like(tiles)
        for b in range(RING):
            for r in range(2):
                at_row = (b % 2) * 2 + r
                tiles[b // 2, at_row : at_row + 1] = scores[b, r : r + 1]
        for side, its_x in ((1, mate), (0, x)):
            for d, (its_z_lo, its_core) in enumerate(group_of):
                if (side, d) != (0, 0):
                    device = at(z_hi, y, its_x, its_z_lo, its_core)
                    send(("out", side, d), tiles.at[side], arrived.at[side, d], device)

    half_a, half_b = pl.ds(0, seq_len // 2), pl.ds(seq_len // 2, seq_len // 2)
    def pass_on(m):
        send(("ra", m), val_in[m].at[0, half_a], relay.at[0, m], to_lo)
        send(("rb", m), val_in[m].at[0, half_b], relay.at[1, m], to_hi)

    own_ready(0, 0)
    pass_on(0)
    pass_on(1)
    own_ready(0, 1)
    for m in range(2):
        for h in range(2):
            send(("x", m, h), train_in[m].at[pl.ds(2 * h, 2)], trains.at[m, pl.ds(4 + 2 * h, 2)], to_mate)
    for copy in local:
        copy.wait()

    seen = set()
    for event in ORDER:
        kind = event[0]
        if kind == "s1":
            act_product(event[1:])
            continue
        if kind == "s2":
            act_cores(event[1:])
            continue
        if kind == "s3":
            act_whole(event[1:])
            continue
        if kind == "s4":
            grad_product(*event[1:])
            continue
        got(event)
        if kind == "ra":
            m = event[1]
            send(("fa", m), relay.at[0, m], vals.at[m, 0, 1, half_a], to_hi)
        elif kind == "rb":
            m = event[1]
            send(("fb", m), relay.at[1, m], vals.at[m, 0, 1, half_b], to_lo)
        elif kind in ("fa", "fb"):
            m = event[1]
            if ("f", m) in seen:
                own_ready(1, m)
            seen.add(("f", m))
        elif kind == "v":
            have(1, *event[1:])
        elif kind == "y":
            q, piece, place = event[1:4]
            if place < 3:
                y_forward(q, piece, place)
                have(q, piece, place)
            elif event[:4] in seen:
                have(q, piece, place)
            seen.add(event[:4])
    out()

    total = tiles[0]
    for side in range(2):
        for d in range(4):
            if (side, d) != (0, 0):
                got(("out", side, d))
                total = total + arrived[side, d]
    out_ref[...] = total[: out_ref.shape[0], : out_ref.shape[1]]
    for copy in copies.values():
        copy.wait_send()


GROUPS = 2 * len(BLOCKS) * len(PLACES)
UNITS = 2 * 4 * 2 * RING
Y_RINGS = sum(1 if first == "y" else 2 for *_, first in PIECES)
V_COPIES = sum(RING if first == "y" else 1 for *_, first in PIECES)
N_COPIES = 8 + 4 + 4 * Y_RINGS + V_COPIES + 3 * GROUPS + 7


def per_device(train_act, train_grad, val_act, val_grad):
    n_train, seq_len, width = train_act.shape
    n_val = lax.axis_size("dp")
    bf16, f32 = train_act.dtype, jnp.float32
    anywhere = pl.BlockSpec(memory_space=pl.ANY)
    coded = (UNITS * seq_len + 16 * GROUPS, seq_len)
    return pl.pallas_call(
        functools.partial(kernel, width * lax.axis_size("tensor")),
        out_shape=jax.ShapeDtypeStruct((n_train, n_val), f32),
        in_specs=[anywhere] * 4,
        out_specs=pl.BlockSpec(memory_space=pltpu.VMEM),
        scratch_shapes=[
            pltpu.VMEM((2, 2 * n_train, seq_len, width), bf16),
            pltpu.VMEM((2, 2 * RING, 2, seq_len, width), bf16),
            pltpu.VMEM((2, 2, seq_len // 2, width), bf16),
            pltpu.VMEM((2, UNITS, seq_len, seq_len), f32),
            pltpu.VMEM((UNITS, seq_len, seq_len), f32),
            pltpu.VMEM(coded, bf16),
            pltpu.VMEM(coded, bf16),
            pltpu.VMEM((2, UNITS, seq_len, seq_len), f32),
            pltpu.VMEM((2 * RING, 2, RING, 2, seq_len), f32),
            pltpu.VMEM((2, 8, 128), f32),
            pltpu.VMEM((2, 4, 8, 128), f32),
            pltpu.SemaphoreType.DMA((4,)),
            pltpu.SemaphoreType.DMA((N_COPIES,)),
            pltpu.SemaphoreType.DMA((N_COPIES,)),
        ],
        compiler_params=pltpu.CompilerParams(
            collective_id=0, has_side_effects=True, vmem_limit_bytes=56 * 1024 * 1024
        ),
        cost_estimate=pl.CostEstimate(
            flops=4 * 32 * (2 * seq_len) ** 2 * width, bytes_accessed=3_300_000, transcendentals=0
        ),
    )(train_act, train_grad, val_act, val_grad)


def solution(mesh):
    placed = P("dp", None, "tensor")
    return jax.shard_map(
        per_device, mesh=mesh, in_specs=(placed,) * 4, out_specs=P("dp", None), check_vma=False
    )
```

```python
import functools

import jax
import jax.numpy as jnp
from jax import lax
from jax.experimental import pallas as pl
from jax.experimental.pallas import tpu as pltpu
from jax.sharding import PartitionSpec as P

MESH = pl.DeviceIdType.MESH
RING = 4

BLOCKS = {"o": (0, 1), "p": (2,), "s": (3,)}
PLACES = {"a": (0,), "b": (1, 2), "c": (3,), "d": (4,), "e": (5, 6), "f": (7,)}

PIECES = (
    (0, 0, 0, 64, "v"),
    (0, 0, 64, 64, "y"),
    (1, 0, 0, 128, "v"),
    (0, 1, 0, 128, "y"),
    (1, 1, 0, 32, "y"),
    (1, 1, 32, 96, "v"),
)

ORDER = (
    ("s1", "o", "a", 0), ("s2", "o", "a", 0), ("v", 0, 0), ("y", 0, 0, 1), ("y", 0, 0, 2), ("ra", 0),
    ("rb", 0), ("v", 1, 0), ("y", 0, 1, 1), ("y", 0, 1, 2), ("ra", 1), ("rb", 1), ("s1", "o", "b", 0),
    ("s3", "o", "a", 0), ("s1", "o", "d", 0), ("y", 1, 0, 1), ("y", 1, 0, 2), ("fa", 0), ("s2", "o", "b", 0),
    ("fb", 0), ("go", 1, 0), ("y", 0, 0, 3, 1), ("y", 0, 0, 3, 2), ("s2", "o", "d", 0), ("s1", "o", "a", 1),
    ("v", 1, 1), ("x", 0, 0), ("go", 0, 1), ("y", 0, 1, 3, 1), ("y", 0, 1, 3, 2), ("fa", 1),
    ("s1", "p", "a", 2), ("s1", "p", "b", 0), ("s1", "o", "c", 0), ("fb", 1), ("y", 1, 0, 3, 1),
    ("y", 1, 0, 3, 2), ("s1", "p", "c", 0), ("s2", "o", "a", 1), ("s1", "p", "d", 0), ("v", 1, 2),
    ("s1", "o", "e", 0), ("s2", "p", "a", 2), ("s2", "p", "b", 0), ("s3", "o", "b", 0), ("s1", "p", "e", 0),
    ("s2", "o", "c", 0), ("s2", "p", "c", 0), ("s3", "o", "d", 0), ("s2", "p", "d", 0), ("s2", "o", "e", 0),
    ("s3", "o", "a", 1), ("s2", "p", "e", 0), ("y", 0, 2, 1), ("y", 0, 2, 2), ("s3", "p", "a", 2),
    ("s1", "o", "b", 1), ("v", 2, 0), ("s3", "p", "b", 0), ("s1", "p", "b", 1), ("s1", "o", "d", 1),
    ("s1", "p", "d", 1), ("s3", "o", "c", 0), ("s3", "p", "c", 0), ("s2", "o", "b", 1), ("s3", "p", "d", 0),
    ("x", 0, 1), ("go", 1, 1), ("s2", "p", "b", 1), ("s2", "o", "d", 1), ("s1", "s", "a", 2),
    ("s2", "p", "d", 1), ("s1", "s", "b", 2), ("y", 0, 3, 1), ("y", 0, 3, 2), ("s3", "o", "e", 0),
    ("s1", "s", "c", 0), ("s1", "s", "d", 2), ("v", 3, 0), ("s1", "s", "e", 0), ("s4", "o", "a"),
    ("s2", "s", "a", 2), ("s3", "p", "e", 0), ("s2", "s", "b", 2), ("y", 0, 2, 3, 1), ("y", 0, 2, 3, 2),
    ("s1", "o", "c", 1), ("s2", "s", "c", 0), ("s2", "s", "d", 2), ("s1", "p", "c", 1), ("v", 1, 3),
    ("s2", "s", "e", 0), ("s3", "o", "b", 1), ("s1", "s", "c", 1), ("s1", "o", "f", 0), ("v", 4, 0),
    ("s3", "p", "b", 1), ("s1", "p", "f", 0), ("s1", "s", "f", 0), ("s2", "o", "c", 1), ("s2", "p", "c", 1),
    ("s3", "o", "d", 1), ("s2", "s", "c", 1), ("s3", "p", "d", 1), ("s2", "o", "f", 0), ("s2", "p", "f", 0),
    ("s3", "s", "a", 2), ("s2", "s", "f", 0), ("y", 1, 2, 1), ("y", 1, 2, 2), ("s1", "o", "e", 1),
    ("v", 5, 0), ("s1", "p", "e", 1), ("x", 1, 0), ("y", 0, 4, 1), ("y", 0, 4, 2), ("s3", "s", "b", 2),
    ("s1", "s", "e", 1), ("s3", "s", "c", 0), ("s4", "o", "d"), ("s4", "p", "a"), ("s2", "o", "e", 1),
    ("s3", "s", "d", 2), ("s2", "p", "e", 1), ("s4", "p", "d"), ("s3", "s", "e", 0), ("s2", "s", "e", 1),
    ("y", 0, 5, 1), ("y", 0, 5, 2), ("s4", "o", "b"), ("v", 3, 1), ("s3", "o", "c", 1), ("s3", "p", "c", 1),
    ("s4", "p", "b"), ("s3", "s", "c", 1), ("y", 0, 3, 3, 1), ("y", 0, 3, 3, 2), ("s3", "o", "f", 0),
    ("s3", "p", "f", 0), ("s3", "s", "f", 0), ("y", 1, 2, 3, 1), ("y", 1, 2, 3, 2), ("s1", "o", "f", 1),
    ("s1", "p", "f", 1), ("s1", "s", "f", 1), ("v", 3, 2), ("s3", "o", "e", 1), ("x", 1, 1), ("s4", "s", "a"),
    ("s4", "s", "b"), ("s3", "p", "e", 1), ("v", 4, 1), ("s4", "s", "d"), ("s2", "o", "f", 1),
    ("s2", "p", "f", 1), ("s2", "s", "f", 1), ("s3", "s", "e", 1), ("v", 4, 2), ("y", 1, 5, 1),
    ("y", 1, 5, 2), ("s4", "o", "e"), ("y", 0, 4, 3, 1), ("y", 0, 4, 3, 2), ("s4", "p", "e"),
    ("s4", "s", "e"), ("y", 0, 5, 3, 1), ("y", 0, 5, 3, 2), ("s3", "o", "f", 1), ("s3", "p", "f", 1),
    ("s4", "o", "c"), ("s3", "s", "f", 1), ("s4", "p", "c"), ("s4", "s", "c"), ("y", 1, 5, 3, 1),
    ("y", 1, 5, 3, 2), ("fold", "a", "b", "c", "d", "e"), ("v", 3, 3), ("v", 4, 3), ("s4", "ops", "f"),
    ("fold", "f"),
)

POWER = 16
PEAK = 222.0


def kernel(
    total_width,
    train_act,
    train_grad,
    val_act,
    val_grad,
    out_ref,
    trains,
    vals,
    relay,
    acts,
    from_core,
    coded_out,
    coded_in,
    whole,
    sums,
    tiles,
    arrived,
    local_sem,
    send_sem,
    recv_sem,
):
    seq_len = train_act.shape[1]
    train_in = (train_act, train_grad)
    val_in = (val_act, val_grad)

    dp = lax.axis_index("dp")
    tensor = lax.axis_index("tensor")
    z_hi, y, x = dp // 16, (dp // 4) % 4, dp % 4
    z_lo, core = tensor // 2, tensor % 2

    def at(z_hi, y, x, z_lo, core):
        return (z_hi * 16 + y * 4 + x, z_lo * 2 + core)

    mate, twin = x + 1 - 2 * (x % 2), 3 - x
    y_at = (y, (y + 3) % 4, (y + 1) % 4, (y + 2) % 4)
    to_y = {1: at(z_hi, y_at[2], x, z_lo, core), 2: at(z_hi, y_at[1], x, z_lo, core)}
    to_mate = at(z_hi, y, mate, z_lo, core)
    to_twin = at(z_hi, y, twin, z_lo, core)
    to_lo = at(z_hi, y, x, 1 - z_lo, core)
    to_hi = at(1 - z_hi, y, x, 1 - z_lo, core)
    to_core = at(z_hi, y, x, z_lo, 1 - core)

    local = []
    for m in range(2):
        local.append(
            pltpu.make_async_copy(train_in[m], trains.at[m, pl.ds(0, 4)], local_sem.at[m])
        )
        local.append(
            pltpu.make_async_copy(val_in[m], vals.at[m, 0, pl.ds(0, 1)], local_sem.at[2 + m])
        )
    for copy in local:
        copy.start()

    barrier = pltpu.get_barrier_semaphore()
    partners = [to_mate, to_twin, to_y[1], to_y[2], to_lo, to_hi, to_core]
    for device in partners:
        pl.semaphore_signal(barrier, inc=1, device_id=device, device_id_type=MESH)
    pl.semaphore_wait(barrier, len(partners))

    copies = {}

    def send(name, src, dst, device):
        key = len(copies)
        copies[name] = pltpu.make_async_remote_copy(
            src_ref=src,
            dst_ref=dst,
            send_sem=send_sem.at[key],
            recv_sem=recv_sem.at[key],
            device_id=device,
            device_id_type=MESH,
        )
        copies[name].start()

    def got(name):
        copies[name].wait_recv()

    def own_val(piece):
        w, m, row, rows, _ = PIECES[piece]
        rows = pl.ds(row, rows)
        return val_in[m].at[0, rows] if w == 0 else vals.at[m, 0, 1, rows]

    def y_direct(q, piece):
        w, m, row, rows, _ = PIECES[piece]
        src = own_val(piece) if q == 0 else vals.at[m, RING, w, pl.ds(row, rows)]
        for place in (1, 2):
            dst = vals.at[m, q * RING + place, w, pl.ds(row, rows)]
            send(("y", q, piece, place), src, dst, to_y[place])

    def y_forward(q, piece, place):
        w, m, row, rows, _ = PIECES[piece]
        half = pl.ds(row + (place - 1) * (rows // 2), rows // 2)
        send(
            ("y", q, piece, 3, place),
            vals.at[m, q * RING + place, w, half],
            vals.at[m, q * RING + 3, w, half],
            to_y[place],
        )

    def v_direct(piece, place):
        w, m, row, rows, _ = PIECES[piece]
        src = own_val(piece) if place == 0 else vals.at[m, place, w, pl.ds(row, rows)]
        send(("v", piece, place), src, vals.at[m, RING + place, w, pl.ds(row, rows)], to_twin)

    def own_ready(w, m):
        for piece, what in enumerate(PIECES):
            if what[:2] == (w, m):
                v_direct(piece, 0)
                y_direct(0, piece)

    def have(q, piece, place):
        first = PIECES[piece][4]
        if first == "y" and q == 0 and place > 0:
            v_direct(piece, place)
        if first == "v" and q == 1 and place == 0:
            y_direct(1, piece)

    starts, rows = {}, {}
    for event in ORDER:
        if event[0] == "s1":
            size = len(BLOCKS[event[1]]) * len(PLACES[event[2]]) * (1 + event[3] // 2)
            first = sum(n for _, n in starts.values())
            rows[event[1:]] = (first * seq_len + 16 * len(starts), size * seq_len + 16)
            starts[event[1:]] = (first, size)

    def act_product(group):
        blocks, places, w = BLOCKS[group[0]], PLACES[group[1]], group[2]
        first, size = starts[group]
        n = len(blocks)
        slots = range(1 + w // 2)

        def one(i, carry):
            right = vals[0, places[0] + i, w] if w < 2 else vals[0, places[0] + i].reshape(2 * seq_len, -1)
            part = lax.dot_general(
                trains[0, 2 * blocks[0] : 2 * blocks[0] + 2 * n].reshape(2 * n * seq_len, -1),
                right,
                (((1,), (1,)), ((), ())),
                preferred_element_type=jnp.float32,
            )
            for k in range(n):
                for r in range(2):
                    at_row = (2 * k + r) * seq_len
                    for j in slots:
                        unit = first + (i * n + k) * len(slots) + j
                        acts[r, unit] = part[at_row : at_row + seq_len, j * seq_len : (j + 1) * seq_len]
            return carry

        lax.fori_loop(0, len(places), one, 0)
        send(("s1",) + group, acts.at[1 - core, pl.ds(first, size)], from_core.at[pl.ds(first, size)], to_core)

    def act_cores(group):
        first, size = starts[group]
        row, n_rows = rows[group]
        got(("s1",) + group)

        def add(i, peak):
            value = acts[core, first + i] + from_core[first + i]
            acts[core, first + i] = value
            return jnp.maximum(peak, jnp.max(jnp.abs(value).reshape(seq_len // 8, 8, seq_len), axis=0))

        peak = lax.fori_loop(0, size, add, jnp.zeros((8, seq_len), jnp.float32))
        peak = jnp.max(jnp.max(peak, axis=0, keepdims=True), axis=1, keepdims=True)
        scale = jnp.broadcast_to(jnp.maximum(peak, 1e-30) * 1.01, (16, seq_len)).astype(jnp.bfloat16)
        coded_out[pl.ds(row + size * seq_len, 16)] = scale
        inverse = PEAK / scale.astype(jnp.float32)[0:1]

        def code(i, carry):
            value = acts[core, first + i]
            power = jnp.abs(value) * inverse
            for _ in range(4):
                power = power * power
            power = jnp.where(value < 0, -power, power).astype(jnp.bfloat16)
            coded_out[pl.ds(pl.multiple_of(row + i * seq_len, 16), seq_len)] = power
            return carry

        lax.fori_loop(0, size, code, 0)
        send(("s2",) + group, coded_out.at[pl.ds(row, n_rows)], coded_in.at[pl.ds(row, n_rows)], to_lo)

    def act_whole(group):
        first, size = starts[group]
        row, _ = rows[group]
        got(("s2",) + group)
        scale = coded_in[pl.ds(row + size * seq_len, 16)].astype(jnp.float32)[0:1] * (1.0 / PEAK)

        def one(i, carry):
            power = coded_in[pl.ds(pl.multiple_of(row + i * seq_len, 16), seq_len)].astype(jnp.float32)
            size_of = jnp.abs(power)
            value = jnp.exp(jnp.log(size_of) * (1.0 / POWER)) * scale
            value = jnp.where(power < 0, -value, value)
            whole[core, first + i] = acts[core, first + i] + jnp.where(size_of > 0, value, 0.0)
            return carry

        lax.fori_loop(0, size, one, 0)
        here = whole.at[core, pl.ds(first, size)]
        send(("s3",) + group, here, here, to_core)

    def grad_product(b_keys, p_key):
        for b_key in b_keys:
            for w in range(3):
                if (b_key, p_key, w) in starts:
                    got(("s3", b_key, p_key, w))

        def one(b_key, i):
            blocks, places = BLOCKS[b_key], PLACES[p_key]
            v, b = places[0] + i // len(blocks), blocks[0] + i % len(blocks)
            part = lax.dot_general(
                trains[1, pl.ds(2 * b, 2)].reshape(2 * seq_len, -1),
                vals[1, v].reshape(2 * seq_len, -1),
                (((1,), (1,)), ((), ())),
                preferred_element_type=jnp.float32,
            )
            for w in range(2):
                if (b_key, p_key, 2) in starts:
                    unit = starts[b_key, p_key, 2][0] + 2 * i + w
                else:
                    unit = starts[b_key, p_key, w][0] + i
                for r in range(2):
                    grad = part[r * seq_len : (r + 1) * seq_len, w * seq_len : (w + 1) * seq_len]
                    total = jnp.sum(whole[r, unit] * grad, axis=0, keepdims=True)
                    sums[v, w, pl.ds(2 * b + r, 1)] = total

        for b_key in b_keys:
            count = len(BLOCKS[b_key]) * len(PLACES[p_key])
            if len(b_keys) > 1:
                for i in range(count):
                    one(b_key, i)
            else:
                lax.fori_loop(0, count, lambda i, carry: (one(b_key, i), carry)[1], 0)

    group_of = ((z_lo, core), (z_lo, 1 - core), (1 - z_lo, core), (1 - z_lo, 1 - core))

    lane = lax.broadcasted_iota(jnp.int32, (8, 128), 1)

    def fold(scores, p_keys):
        for v in [v for p_key in p_keys for v in PLACES[p_key]]:
            for w in range(2):
                its_z_hi = z_hi if w == 0 else 1 - z_hi
                column = its_z_hi * 16 + y_at[v % RING] * 4 + (x if v < RING else twin)
                scores = jnp.where(lane == column, jnp.sum(sums[v, w], axis=1, keepdims=True), scores)
        return scores

    def out(scores):
        scores = scores * (1.0 / (total_width * seq_len))
        tiles[0, 0:4] = scores[0:4]
        tiles[1, 0:4] = scores[4:8]
        for side, its_x in ((1, mate), (0, x)):
            for d, (its_z_lo, its_core) in enumerate(group_of):
                if (side, d) != (0, 0):
                    device = at(z_hi, y, its_x, its_z_lo, its_core)
                    send(("out", side, d), tiles.at[side], arrived.at[side, d], device)

    half_a, half_b = pl.ds(0, seq_len // 2), pl.ds(seq_len // 2, seq_len // 2)
    def pass_on(m):
        send(("ra", m), val_in[m].at[0, half_a], relay.at[0, m], to_lo)
        send(("rb", m), val_in[m].at[0, half_b], relay.at[1, m], to_hi)

    own_ready(0, 0)
    pass_on(0)
    pass_on(1)
    for m in range(2):
        for h in range(2):
            send(("x", m, h), train_in[m].at[pl.ds(2 * h, 2)], trains.at[m, pl.ds(4 + 2 * h, 2)], to_mate)
    for copy in local:
        copy.wait()

    seen = set()
    scores = jnp.zeros((8, 128), jnp.float32)
    for event in ORDER:
        kind = event[0]
        if kind == "go":
            own_ready(*event[1:])
            continue
        if kind == "fold":
            scores = fold(scores, event[1:])
            continue
        if kind == "s1":
            act_product(event[1:])
            continue
        if kind == "s2":
            act_cores(event[1:])
            continue
        if kind == "s3":
            act_whole(event[1:])
            continue
        if kind == "s4":
            grad_product(*event[1:])
            continue
        got(event)
        if kind == "ra":
            m = event[1]
            send(("fa", m), relay.at[0, m], vals.at[m, 0, 1, half_a], to_hi)
        elif kind == "rb":
            m = event[1]
            send(("fb", m), relay.at[1, m], vals.at[m, 0, 1, half_b], to_lo)
        elif kind in ("fa", "fb"):
            pass
        elif kind == "v":
            have(1, *event[1:])
        elif kind == "y":
            q, piece, place = event[1:4]
            if place < 3:
                y_forward(q, piece, place)
                have(q, piece, place)
            elif event[:4] in seen:
                have(q, piece, place)
            seen.add(event[:4])
    out(scores)

    total = tiles[0, 0:4]
    for side in range(2):
        for d in range(4):
            if (side, d) != (0, 0):
                got(("out", side, d))
                total = total + arrived[side, d, 0:4]
    out_ref[...] = total[:, : out_ref.shape[1]]
    for copy in copies.values():
        copy.wait_send()


GROUPS = sum(1 for event in ORDER if event[0] == "s1")
UNITS = 2 * 4 * 2 * RING
Y_RINGS = sum(1 if first == "y" else 2 for *_, first in PIECES)
V_COPIES = sum(RING if first == "y" else 1 for *_, first in PIECES)
N_COPIES = 8 + 4 + 4 * Y_RINGS + V_COPIES + 3 * GROUPS + 7


def per_device(train_act, train_grad, val_act, val_grad):
    n_train, seq_len, width = train_act.shape
    n_val = lax.axis_size("dp")
    bf16, f32 = train_act.dtype, jnp.float32
    anywhere = pl.BlockSpec(memory_space=pl.ANY)
    coded = (UNITS * seq_len + 16 * GROUPS, seq_len)
    return pl.pallas_call(
        functools.partial(kernel, width * lax.axis_size("tensor")),
        out_shape=jax.ShapeDtypeStruct((n_train, n_val), f32),
        in_specs=[anywhere] * 4,
        out_specs=pl.BlockSpec(memory_space=pltpu.VMEM),
        scratch_shapes=[
            pltpu.VMEM((2, 2 * n_train, seq_len, width), bf16),
            pltpu.VMEM((2, 2 * RING, 2, seq_len, width), bf16),
            pltpu.VMEM((2, 2, seq_len // 2, width), bf16),
            pltpu.VMEM((2, UNITS, seq_len, seq_len), f32),
            pltpu.VMEM((UNITS, seq_len, seq_len), f32),
            pltpu.VMEM(coded, bf16),
            pltpu.VMEM(coded, bf16),
            pltpu.VMEM((2, UNITS, seq_len, seq_len), f32),
            pltpu.VMEM((2 * RING, 2, 8, seq_len), f32),
            pltpu.VMEM((2, 8, 128), f32),
            pltpu.VMEM((2, 4, 8, 128), f32),
            pltpu.SemaphoreType.DMA((4,)),
            pltpu.SemaphoreType.DMA((N_COPIES,)),
            pltpu.SemaphoreType.DMA((N_COPIES,)),
        ],
        compiler_params=pltpu.CompilerParams(
            collective_id=0, has_side_effects=True, vmem_limit_bytes=56 * 1024 * 1024
        ),
        cost_estimate=pl.CostEstimate(
            flops=4 * 32 * (2 * seq_len) ** 2 * width, bytes_accessed=3_300_000, transcendentals=0
        ),
    )(train_act, train_grad, val_act, val_grad)


def solution(mesh):
    placed = P("dp", None, "tensor")
    return jax.shard_map(
        per_device, mesh=mesh, in_specs=(placed,) * 4, out_specs=P("dp", None), check_vma=False
    )
```

```python
import functools

import jax
import jax.numpy as jnp
from jax import lax
from jax.experimental import pallas as pl
from jax.experimental.pallas import tpu as pltpu
from jax.sharding import PartitionSpec as P

MESH = pl.DeviceIdType.MESH
LAST = "f"
RING = 4

BLOCKS = {"o": (0, 1), "p": (2,), "s": (3,)}
PLACES = {"a": (0,), "b": (1, 2), "c": (3,), "d": (4,), "e": (5, 6), "f": (7,)}

PIECES = (
    (0, 0, 0, 64, "v"),
    (0, 0, 64, 64, "y"),
    (1, 0, 0, 128, "v"),
    (0, 1, 0, 32, "y"),
    (0, 1, 32, 96, "y"),
    (1, 1, 0, 32, "y"),
    (1, 1, 32, 96, "v"),
)
AT_ONCE = (0, 1)

EARLY = (3,)
ORDER = (
    ("v", 0, 0), ("y", 0, 0, 1), ("y", 0, 0, 2), ("ra", 0), ("rb", 0), ("go", 3), ("s1", "o", "a", 0),
    ("v", 1, 0), ("y", 0, 1, 1), ("y", 0, 1, 2), ("ra", 1), ("rb", 1), ("s1", "o", "b", 0), ("v", 3, 0),
    ("s2", "o", "a", 0), ("s1", "o", "d", 0), ("y", 1, 0, 1), ("y", 1, 0, 2), ("fa", 0), ("fb", 0), ("go", 2),
    ("s1", "o", "a", 1), ("s2", "o", "b", 0), ("y", 0, 0, 3, 1), ("y", 0, 0, 3, 2), ("s2", "o", "d", 0),
    ("v", 1, 1), ("x", 0, 0), ("s1", "p", "a", 2), ("fa", 1), ("fb", 1), ("go", 5), ("y", 0, 3, 1),
    ("y", 0, 3, 2), ("s2", "o", "a", 1), ("s1", "p", "b", 0), ("s3", "o", "a", 0), ("s1", "p", "d", 0),
    ("y", 0, 1, 3, 1), ("y", 0, 1, 3, 2), ("s1", "op", "c", 0), ("v", 1, 2), ("s2", "p", "a", 2),
    ("s1", "op", "e", 0), ("y", 1, 0, 3, 1), ("y", 1, 0, 3, 2), ("s2", "p", "b", 0), ("s2", "p", "d", 0),
    ("s3", "o", "b", 0), ("s2", "op", "c", 0), ("s3", "o", "d", 0), ("s3", "o", "a", 1), ("s2", "op", "e", 0),
    ("s3", "p", "a", 2), ("v", 2, 0), ("s1", "op", "d", 1), ("y", 0, 2, 1), ("y", 0, 2, 2),
    ("s3", "p", "b", 0), ("s1", "op", "b", 1), ("v", 5, 0), ("y", 0, 5, 1), ("y", 0, 5, 2), ("go", 4),
    ("y", 0, 3, 3, 1), ("y", 0, 3, 3, 2), ("v", 3, 1), ("x", 0, 1), ("s2", "op", "d", 1), ("s3", "p", "d", 0),
    ("s3", "op", "c", 0), ("s1", "s", "a", 2), ("s1", "s", "b", 2), ("v", 3, 2), ("s1", "s", "c", 0),
    ("s1", "s", "d", 2), ("s2", "op", "b", 1), ("s4", "o", "a"), ("s2", "s", "a", 2), ("s3", "op", "e", 0),
    ("s2", "s", "b", 2), ("s2", "s", "c", 0), ("v", 1, 3), ("s2", "s", "d", 2), ("s3", "op", "d", 1),
    ("y", 1, 2, 1), ("y", 1, 2, 2), ("v", 5, 1), ("s1", "s", "e", 2), ("s1", "op", "e", 1), ("v", 5, 2),
    ("y", 0, 2, 3, 1), ("go", 6), ("y", 0, 2, 3, 2), ("s1", "ops", "c", 1), ("y", 0, 5, 3, 1),
    ("y", 0, 5, 3, 2), ("s2", "s", "e", 2), ("s3", "op", "b", 1), ("s2", "op", "e", 1), ("s3", "s", "a", 2),
    ("x", 1, 0), ("s4", "p", "a"), ("v", 4, 0), ("s2", "ops", "c", 1), ("s3", "s", "b", 2), ("v", 3, 3),
    ("s3", "s", "c", 0), ("y", 0, 4, 1), ("y", 0, 4, 2), ("s3", "s", "d", 2), ("y", 1, 2, 3, 1),
    ("y", 1, 2, 3, 2), ("s1", "o", "f", 2), ("s1", "p", "f", 2), ("s3", "s", "e", 2), ("v", 6, 0),
    ("s1", "s", "f", 2), ("s4", "o", "d"), ("s4", "p", "d"), ("v", 5, 3), ("s2", "o", "f", 2),
    ("s2", "p", "f", 2), ("s2", "s", "f", 2), ("s3", "op", "e", 1), ("y", 0, 6, 1), ("y", 0, 6, 2),
    ("s4", "o", "b"), ("s4", "p", "b"), ("x", 1, 1), ("y", 0, 4, 3, 1), ("y", 0, 4, 3, 2), ("v", 4, 1),
    ("s3", "ops", "c", 1), ("s4", "s", "a"), ("fold", "a"), ("s4", "s", "b"), ("fold", "b"), ("s4", "s", "d"),
    ("fold", "d"), ("s3", "o", "f", 2), ("s3", "p", "f", 2), ("y", 1, 6, 1), ("y", 1, 6, 2), ("v", 4, 2),
    ("s4", "o", "e"), ("s3", "s", "f", 2), ("s4", "p", "e"), ("y", 0, 6, 3, 1), ("y", 0, 6, 3, 2),
    ("s4", "o", "c"), ("s4", "p", "c"), ("s4", "s", "c"), ("s4", "s", "e"), ("y", 1, 6, 3, 1), ("v", 4, 3),
    ("y", 1, 6, 3, 2), ("fold", "c", "e"), ("s4", "ps", "f"), ("fold1", "f"), ("out", 1), ("s4", "o", "f"),
    ("fold0", "f"), ("out", 0),
)

POWER = 16
PEAK = 222.0


def kernel(
    total_width,
    train_act,
    train_grad,
    val_act,
    val_grad,
    out_ref,
    trains,
    vals,
    relay,
    acts,
    from_core,
    coded_out,
    coded_in,
    whole,
    sums,
    tiles,
    arrived,
    result,
    local_sem,
    send_sem,
    recv_sem,
):
    seq_len = train_act.shape[1]
    train_in = (train_act, train_grad)
    val_in = (val_act, val_grad)

    dp = lax.axis_index("dp")
    tensor = lax.axis_index("tensor")
    z_hi, y, x = dp // 16, (dp // 4) % 4, dp % 4
    z_lo, core = tensor // 2, tensor % 2

    def at(z_hi, y, x, z_lo, core):
        return (z_hi * 16 + y * 4 + x, z_lo * 2 + core)

    mate, twin = x + 1 - 2 * (x % 2), 3 - x
    y_at = (y, (y + 3) % 4, (y + 1) % 4, (y + 2) % 4)
    to_y = {1: at(z_hi, y_at[2], x, z_lo, core), 2: at(z_hi, y_at[1], x, z_lo, core)}
    to_mate = at(z_hi, y, mate, z_lo, core)
    to_twin = at(z_hi, y, twin, z_lo, core)
    to_lo = at(z_hi, y, x, 1 - z_lo, core)
    to_hi = at(1 - z_hi, y, x, 1 - z_lo, core)
    to_core = at(z_hi, y, x, z_lo, 1 - core)

    local = []
    for m in range(2):
        local.append(
            pltpu.make_async_copy(train_in[m], trains.at[m, pl.ds(0, 4)], local_sem.at[m])
        )
        local.append(
            pltpu.make_async_copy(val_in[m], vals.at[m, 0, pl.ds(0, 1)], local_sem.at[2 + m])
        )
    for copy in local:
        copy.start()

    barrier = pltpu.get_barrier_semaphore()
    partners = [to_mate, to_twin, to_y[1], to_y[2], to_lo, to_hi, to_core]
    for device in partners:
        pl.semaphore_signal(barrier, inc=1, device_id=device, device_id_type=MESH)
    pl.semaphore_wait(barrier, len(partners))

    copies = {}

    def send(name, src, dst, device):
        key = len(copies)
        copies[name] = pltpu.make_async_remote_copy(
            src_ref=src,
            dst_ref=dst,
            send_sem=send_sem.at[key],
            recv_sem=recv_sem.at[key],
            device_id=device,
            device_id_type=MESH,
        )
        copies[name].start()

    def got(name):
        copies[name].wait_recv()

    def own_val(piece):
        w, m, row, rows, _ = PIECES[piece]
        rows = pl.ds(row, rows)
        return val_in[m].at[0, rows] if w == 0 else vals.at[m, 0, 1, rows]

    def y_direct(q, piece):
        w, m, row, rows, _ = PIECES[piece]
        src = own_val(piece) if q == 0 else vals.at[m, RING, w, pl.ds(row, rows)]
        for place in (1, 2):
            dst = vals.at[m, q * RING + place, w, pl.ds(row, rows)]
            send(("y", q, piece, place), src, dst, to_y[place])

    def y_forward(q, piece, place):
        w, m, row, rows, _ = PIECES[piece]
        half = pl.ds(row + (place - 1) * (rows // 2), rows // 2)
        send(
            ("y", q, piece, 3, place),
            vals.at[m, q * RING + place, w, half],
            vals.at[m, q * RING + 3, w, half],
            to_y[place],
        )

    def v_direct(piece, place):
        w, m, row, rows, _ = PIECES[piece]
        src = own_val(piece) if place == 0 else vals.at[m, place, w, pl.ds(row, rows)]
        send(("v", piece, place), src, vals.at[m, RING + place, w, pl.ds(row, rows)], to_twin)

    def own_ready(piece):
        if piece not in EARLY:
            v_direct(piece, 0)
        y_direct(0, piece)

    def have(q, piece, place):
        first = PIECES[piece][4]
        if first == "y" and q == 0 and place > 0:
            v_direct(piece, place)
        if first == "v" and q == 1 and place == 0:
            y_direct(1, piece)

    def blocks_of(keys):
        return [b for key in keys for b in BLOCKS[key]]

    starts, rows = {}, {}
    for event in ORDER:
        if event[0] == "s1":
            size = len(blocks_of(event[1])) * len(PLACES[event[2]]) * (1 + event[3] // 2)
            first = sum(n for _, n in starts.values())
            rows[event[1:]] = (first * seq_len + 16 * len(starts), size * seq_len + 16)
            starts[event[1:]] = (first, size)

    def act_product(group):
        blocks, places, w = blocks_of(group[0]), PLACES[group[1]], group[2]
        first, size = starts[group]
        n = len(blocks)
        slots = range(1 + w // 2)

        def one(i, carry):
            right = vals[0, places[0] + i, w] if w < 2 else vals[0, places[0] + i].reshape(2 * seq_len, -1)
            part = lax.dot_general(
                trains[0, 2 * blocks[0] : 2 * blocks[0] + 2 * n].reshape(2 * n * seq_len, -1),
                right,
                (((1,), (1,)), ((), ())),
                preferred_element_type=jnp.float32,
            )
            for k in range(n):
                for r in range(2):
                    at_row = (2 * k + r) * seq_len
                    for j in slots:
                        unit = first + (i * n + k) * len(slots) + j
                        acts[r, unit] = part[at_row : at_row + seq_len, j * seq_len : (j + 1) * seq_len]
            return carry

        lax.fori_loop(0, len(places), one, 0)
        send(("s1",) + group, acts.at[1 - core, pl.ds(first, size)], from_core.at[pl.ds(first, size)], to_core)

    def act_cores(group):
        first, size = starts[group]
        row, n_rows = rows[group]
        got(("s1",) + group)

        def add(i, peak):
            value = acts[core, first + i] + from_core[first + i]
            acts[core, first + i] = value
            return jnp.maximum(peak, jnp.max(jnp.abs(value).reshape(seq_len // 8, 8, seq_len), axis=0))

        peak = lax.fori_loop(0, size, add, jnp.zeros((8, seq_len), jnp.float32))
        peak = jnp.max(jnp.max(peak, axis=0, keepdims=True), axis=1, keepdims=True)
        scale = jnp.broadcast_to(jnp.maximum(peak, 1e-30) * 1.01, (16, seq_len)).astype(jnp.bfloat16)
        coded_out[pl.ds(row + size * seq_len, 16)] = scale
        inverse = PEAK / scale.astype(jnp.float32)[0:1]

        def code(i, carry):
            value = acts[core, first + i]
            power = jnp.abs(value) * inverse
            for _ in range(4):
                power = power * power
            power = jnp.where(value < 0, -power, power).astype(jnp.bfloat16)
            coded_out[pl.ds(pl.multiple_of(row + i * seq_len, 16), seq_len)] = power
            return carry

        lax.fori_loop(0, size, code, 0)
        send(("s2",) + group, coded_out.at[pl.ds(row, n_rows)], coded_in.at[pl.ds(row, n_rows)], to_lo)

    def act_whole(group):
        first, size = starts[group]
        row, _ = rows[group]
        got(("s2",) + group)
        scale = coded_in[pl.ds(row + size * seq_len, 16)].astype(jnp.float32)[0:1] * (1.0 / PEAK)

        def one(i, carry):
            power = coded_in[pl.ds(pl.multiple_of(row + i * seq_len, 16), seq_len)].astype(jnp.float32)
            size_of = jnp.abs(power)
            value = jnp.exp(jnp.log(size_of) * (1.0 / POWER)) * scale
            value = jnp.where(power < 0, -value, value)
            whole[core, first + i] = acts[core, first + i] + jnp.where(size_of > 0, value, 0.0)
            return carry

        lax.fori_loop(0, size, one, 0)
        here = whole.at[core, pl.ds(first, size)]
        send(("s3",) + group, here, here, to_core)

    arrived_acts = set()

    def grad_product(b_keys, p_key):
        acts_of = {}
        for b_key in b_keys:
            for group in starts:
                if b_key in group[0] and p_key == group[1]:
                    if group not in arrived_acts:
                        arrived_acts.add(group)
                        got(("s3",) + group)
                    for w in range(2):
                        if group[2] in (w, 2):
                            acts_of[b_key, w] = group

        def one(b_key, i):
            blocks, places = BLOCKS[b_key], PLACES[p_key]
            v, b = places[0] + i // len(blocks), blocks[0] + i % len(blocks)
            part = lax.dot_general(
                trains[1, pl.ds(2 * b, 2)].reshape(2 * seq_len, -1),
                vals[1, v].reshape(2 * seq_len, -1),
                (((1,), (1,)), ((), ())),
                preferred_element_type=jnp.float32,
            )
            for w in range(2):
                group = acts_of[b_key, w]
                in_group = blocks_of(group[0])
                unit = i // len(blocks) * len(in_group) + b - in_group[0]
                if group[2] == 2:
                    unit = 2 * unit + w
                unit = starts[group][0] + unit
                for r in range(2):
                    grad = part[r * seq_len : (r + 1) * seq_len, w * seq_len : (w + 1) * seq_len]
                    total = jnp.sum(whole[r, unit] * grad, axis=0, keepdims=True)
                    sums[b // 2, v, w, pl.ds(2 * (b % 2) + r, 1)] = total

        for b_key in b_keys:
            count = len(BLOCKS[b_key]) * len(PLACES[p_key])
            if p_key == LAST:
                for i in range(count):
                    one(b_key, i)
            else:
                lax.fori_loop(0, count, lambda i, carry: (one(b_key, i), carry)[1], 0)

    group_of = ((z_lo, core), (z_lo, 1 - core), (1 - z_lo, core), (1 - z_lo, 1 - core))

    lane = lax.broadcasted_iota(jnp.int32, (4, 128), 1)

    def fold(side, p_keys):
        for v in [v for p_key in p_keys for v in PLACES[p_key]]:
            for w in range(2):
                its_z_hi = z_hi if w == 0 else 1 - z_hi
                column = its_z_hi * 16 + y_at[v % RING] * 4 + (x if v < RING else twin)
                total = jnp.sum(sums[side, v, w], axis=1, keepdims=True)
                scores[side] = jnp.where(lane == column, total, scores[side])

    def out(side):
        tiles[side, 0:4] = scores[side] * (1.0 / (total_width * seq_len))
        for d in (3, 2, 1, 0):
            its_z_lo, its_core = group_of[d]
            if (side, d) != (0, 0):
                device = at(z_hi, y, (x, mate)[side], its_z_lo, its_core)
                send(("out", side, d), tiles.at[side], arrived.at[side, d], device)

    half_a, half_b = pl.ds(0, seq_len // 2), pl.ds(seq_len // 2, seq_len // 2)
    def pass_on(m):
        send(("ra", m), val_in[m].at[0, half_a], relay.at[0, m], to_lo)
        send(("rb", m), val_in[m].at[0, half_b], relay.at[1, m], to_hi)

    for piece in AT_ONCE:
        own_ready(piece)
    for m in range(2):
        pass_on(m)
    for piece in EARLY:
        v_direct(piece, 0)
    for m in range(2):
        for h in range(2):
            send(("x", m, h), train_in[m].at[pl.ds(2 * h, 2)], trains.at[m, pl.ds(4 + 2 * h, 2)], to_mate)
    for copy in local:
        copy.wait()

    seen = set()
    scores = [jnp.zeros((4, 128), jnp.float32)] * 2
    for event in ORDER:
        kind = event[0]
        if kind == "go":
            own_ready(*event[1:])
            continue
        if kind.startswith("fold"):
            for side in range(2):
                if kind != ("fold1", "fold0")[side]:
                    fold(side, event[1:])
            continue
        if kind == "out":
            out(event[1])
            continue
        if kind == "s1":
            act_product(event[1:])
            continue
        if kind == "s2":
            act_cores(event[1:])
            continue
        if kind == "s3":
            act_whole(event[1:])
            continue
        if kind == "s4":
            grad_product(*event[1:])
            continue
        got(event)
        if kind == "ra":
            m = event[1]
            send(("fa", m), relay.at[0, m], vals.at[m, 0, 1, half_a], to_hi)
        elif kind == "rb":
            m = event[1]
            send(("fb", m), relay.at[1, m], vals.at[m, 0, 1, half_b], to_lo)
        elif kind == "v":
            have(1, *event[1:])
        elif kind == "y":
            q, piece, place = event[1:4]
            if place < 3:
                y_forward(q, piece, place)
                have(q, piece, place)
            elif event[:4] in seen:
                have(q, piece, place)
            seen.add(event[:4])
    total = tiles[0, 0:4]
    for side in range(2):
        for d in range(4):
            if (side, d) != (0, 0):
                got(("out", side, d))
                total = total + arrived[side, d, 0:4]
    result[...] = total[:, : out_ref.shape[1]]
    copy_out = pltpu.make_async_copy(result, out_ref, local_sem.at[0])
    copy_out.start()
    for copy in copies.values():
        copy.wait_send()
    copy_out.wait()


GROUPS = sum(1 for event in ORDER if event[0] == "s1")
UNITS = 2 * 4 * 2 * RING
Y_RINGS = sum(1 if first == "y" else 2 for *_, first in PIECES)
V_COPIES = sum(RING if first == "y" else 1 for *_, first in PIECES)
N_COPIES = 8 + 4 + 4 * Y_RINGS + V_COPIES + 3 * GROUPS + 7


def per_device(train_act, train_grad, val_act, val_grad):
    n_train, seq_len, width = train_act.shape
    n_val = lax.axis_size("dp")
    bf16, f32 = train_act.dtype, jnp.float32
    anywhere = pl.BlockSpec(memory_space=pl.ANY)
    coded = (UNITS * seq_len + 16 * GROUPS, seq_len)
    return pl.pallas_call(
        functools.partial(kernel, width * lax.axis_size("tensor")),
        out_shape=jax.ShapeDtypeStruct((n_train, n_val), f32),
        in_specs=[anywhere] * 4,
        out_specs=anywhere,
        scratch_shapes=[
            pltpu.VMEM((2, 2 * n_train, seq_len, width), bf16),
            pltpu.VMEM((2, 2 * RING, 2, seq_len, width), bf16),
            pltpu.VMEM((2, 2, seq_len // 2, width), bf16),
            pltpu.VMEM((2, UNITS, seq_len, seq_len), f32),
            pltpu.VMEM((UNITS, seq_len, seq_len), f32),
            pltpu.VMEM(coded, bf16),
            pltpu.VMEM(coded, bf16),
            pltpu.VMEM((2, UNITS, seq_len, seq_len), f32),
            pltpu.VMEM((2, 2 * RING, 2, 4, seq_len), f32),
            pltpu.VMEM((2, 8, 128), f32),
            pltpu.VMEM((2, 4, 8, 128), f32),
            pltpu.VMEM((n_train, n_val), f32),
            pltpu.SemaphoreType.DMA((4,)),
            pltpu.SemaphoreType.DMA((N_COPIES,)),
            pltpu.SemaphoreType.DMA((N_COPIES,)),
        ],
        compiler_params=pltpu.CompilerParams(
            collective_id=0, has_side_effects=True, vmem_limit_bytes=56 * 1024 * 1024
        ),
        cost_estimate=pl.CostEstimate(
            flops=4 * 32 * (2 * seq_len) ** 2 * width, bytes_accessed=3_300_000, transcendentals=0
        ),
    )(train_act, train_grad, val_act, val_grad)


def solution(mesh):
    placed = P("dp", None, "tensor")
    return jax.shard_map(
        per_device, mesh=mesh, in_specs=(placed,) * 4, out_specs=P("dp", None), check_vma=False
    )
```

```python
import functools

import jax
import jax.numpy as jnp
from jax import lax
from jax.experimental import pallas as pl
from jax.experimental.pallas import tpu as pltpu
from jax.sharding import PartitionSpec as P

MESH = pl.DeviceIdType.MESH
LAST = "f"
RING = 4

BLOCKS = {"o": (0, 1), "p": (2,), "s": (3,)}
PLACES = {"a": (0,), "b": (1, 2), "c": (3,), "d": (4,), "e": (5, 6), "f": (7,)}

PIECES = (
    (0, 0, 0, 64, "v"),
    (0, 0, 64, 64, "y"),
    (1, 0, 0, 128, "v"),
    (0, 1, 0, 32, "y"),
    (0, 1, 32, 96, "y"),
    (1, 1, 0, 32, "y"),
    (1, 1, 32, 96, "v"),
)
AT_ONCE = (0, 1)

EARLY = (3,)
ORDER = (
    ("v", 0, 0), ("y", 0, 0, 1), ("y", 0, 0, 2), ("ra", 0), ("rb", 0), ("go", 3), ("s1", "o", "a", 0),
    ("v", 1, 0), ("y", 0, 1, 1), ("y", 0, 1, 2), ("ra", 1), ("rb", 1), ("s1", "o", "b", 0), ("v", 3, 0),
    ("s2", "o", "a", 0), ("s1", "o", "d", 0), ("y", 1, 0, 1), ("y", 1, 0, 2), ("fa", 0), ("fb", 0), ("go", 2),
    ("s1", "o", "a", 1), ("s2", "o", "b", 0), ("y", 0, 0, 3, 1), ("y", 0, 0, 3, 2), ("s2", "o", "d", 0),
    ("v", 1, 1), ("x", 0, 0), ("s1", "p", "a", 2), ("fa", 1), ("fb", 1), ("go", 5), ("y", 0, 3, 1),
    ("y", 0, 3, 2), ("s2", "o", "a", 1), ("s1", "p", "b", 0), ("s3", "o", "a", 0), ("s1", "p", "d", 0),
    ("y", 0, 1, 3, 1), ("y", 0, 1, 3, 2), ("s1", "op", "c", 0), ("v", 1, 2), ("s2", "p", "a", 2),
    ("s1", "op", "e", 0), ("y", 1, 0, 3, 1), ("y", 1, 0, 3, 2), ("s2", "p", "b", 0), ("s2", "p", "d", 0),
    ("s3", "o", "b", 0), ("s2", "op", "c", 0), ("s3", "o", "d", 0), ("s3", "o", "a", 1), ("s2", "op", "e", 0),
    ("s3", "p", "a", 2), ("v", 2, 0), ("s1", "op", "d", 1), ("y", 0, 2, 1), ("y", 0, 2, 2),
    ("s3", "p", "b", 0), ("s1", "op", "b", 1), ("v", 5, 0), ("y", 0, 5, 1), ("y", 0, 5, 2), ("go", 4),
    ("y", 0, 3, 3, 1), ("y", 0, 3, 3, 2), ("v", 3, 1), ("x", 0, 1), ("s2", "op", "d", 1), ("s3", "p", "d", 0),
    ("s3", "op", "c", 0), ("s1", "s", "a", 2), ("s1", "s", "b", 2), ("v", 3, 2), ("s1", "s", "c", 0),
    ("s1", "s", "d", 2), ("s2", "op", "b", 1), ("s4", "o", "a"), ("s2", "s", "a", 2), ("s3", "op", "e", 0),
    ("s2", "s", "b", 2), ("s2", "s", "c", 0), ("v", 1, 3), ("s2", "s", "d", 2), ("s3", "op", "d", 1),
    ("y", 1, 2, 1), ("y", 1, 2, 2), ("v", 5, 1), ("s1", "s", "e", 2), ("s1", "op", "e", 1), ("v", 5, 2),
    ("y", 0, 2, 3, 1), ("go", 6), ("y", 0, 2, 3, 2), ("s1", "ops", "c", 1), ("y", 0, 5, 3, 1),
    ("y", 0, 5, 3, 2), ("s2", "s", "e", 2), ("s3", "op", "b", 1), ("s2", "op", "e", 1), ("s3", "s", "a", 2),
    ("x", 1, 0), ("s4", "p", "a"), ("v", 4, 0), ("s2", "ops", "c", 1), ("s3", "s", "b", 2), ("v", 3, 3),
    ("s3", "s", "c", 0), ("y", 0, 4, 1), ("y", 0, 4, 2), ("s3", "s", "d", 2), ("y", 1, 2, 3, 1),
    ("y", 1, 2, 3, 2), ("s1", "o", "f", 2), ("s1", "p", "f", 2), ("s3", "s", "e", 2), ("v", 6, 0),
    ("s1", "s", "f", 2), ("s4", "o", "d"), ("s4", "p", "d"), ("v", 5, 3), ("s2", "o", "f", 2),
    ("s2", "p", "f", 2), ("s2", "s", "f", 2), ("s3", "op", "e", 1), ("y", 0, 6, 1), ("y", 0, 6, 2),
    ("s4", "o", "b"), ("s4", "p", "b"), ("x", 1, 1), ("y", 0, 4, 3, 1), ("y", 0, 4, 3, 2), ("v", 4, 1),
    ("s3", "ops", "c", 1), ("s4", "s", "a"), ("fold", "a"), ("s4", "s", "b"), ("fold", "b"), ("s4", "s", "d"),
    ("fold", "d"), ("s3", "o", "f", 2), ("s3", "p", "f", 2), ("y", 1, 6, 1), ("y", 1, 6, 2), ("v", 4, 2),
    ("s4", "o", "e"), ("s3", "s", "f", 2), ("s4", "p", "e"), ("y", 0, 6, 3, 1), ("y", 0, 6, 3, 2),
    ("s4", "o", "c"), ("s4", "p", "c"), ("s4", "s", "c"), ("s4", "s", "e"), ("y", 1, 6, 3, 1), ("v", 4, 3),
    ("y", 1, 6, 3, 2), ("fold", "c", "e"), ("s4", "ps", "f"), ("fold1", "f"), ("out", 1), ("s4", "o", "f"),
    ("fold0", "f"), ("out", 0),
)

POWER = 16
PEAK = 222.0


def kernel(
    total_width,
    train_act,
    train_grad,
    val_act,
    val_grad,
    out_ref,
    trains,
    vals,
    relay,
    acts,
    from_core,
    coded_out,
    coded_in,
    whole,
    sums,
    tiles,
    arrived,
    result,
    local_sem,
    send_sem,
    recv_sem,
):
    seq_len = train_act.shape[1]
    train_in = (train_act, train_grad)
    val_in = (val_act, val_grad)

    dp = lax.axis_index("dp")
    tensor = lax.axis_index("tensor")
    z_hi, y, x = dp // 16, (dp // 4) % 4, dp % 4
    z_lo, core = tensor // 2, tensor % 2

    def at(z_hi, y, x, z_lo, core):
        return (z_hi * 16 + y * 4 + x, z_lo * 2 + core)

    mate, twin = x + 1 - 2 * (x % 2), 3 - x
    y_at = (y, (y + 3) % 4, (y + 1) % 4, (y + 2) % 4)
    to_y = {1: at(z_hi, y_at[2], x, z_lo, core), 2: at(z_hi, y_at[1], x, z_lo, core)}
    to_mate = at(z_hi, y, mate, z_lo, core)
    to_twin = at(z_hi, y, twin, z_lo, core)
    to_lo = at(z_hi, y, x, 1 - z_lo, core)
    to_hi = at(1 - z_hi, y, x, 1 - z_lo, core)
    to_core = at(z_hi, y, x, z_lo, 1 - core)

    local = []
    for m in range(2):
        local.append(
            pltpu.make_async_copy(train_in[m], trains.at[m, pl.ds(0, 4)], local_sem.at[m])
        )
        local.append(
            pltpu.make_async_copy(val_in[m], vals.at[m, 0, pl.ds(0, 1)], local_sem.at[2 + m])
        )
    for copy in local:
        copy.start()

    barrier = pltpu.get_barrier_semaphore()
    partners = [to_mate, to_twin, to_y[1], to_y[2], to_lo, to_hi, to_core]
    for device in partners:
        pl.semaphore_signal(barrier, inc=1, device_id=device, device_id_type=MESH)
    pl.semaphore_wait(barrier, len(partners))

    copies = {}

    def send(name, src, dst, device):
        key = len(copies)
        copies[name] = pltpu.make_async_remote_copy(
            src_ref=src,
            dst_ref=dst,
            send_sem=send_sem.at[key],
            recv_sem=recv_sem.at[key],
            device_id=device,
            device_id_type=MESH,
        )
        copies[name].start()

    def got(name):
        copies[name].wait_recv()

    def own_val(piece):
        w, m, row, rows, _ = PIECES[piece]
        rows = pl.ds(row, rows)
        return val_in[m].at[0, rows] if w == 0 else vals.at[m, 0, 1, rows]

    def y_direct(q, piece):
        w, m, row, rows, _ = PIECES[piece]
        src = own_val(piece) if q == 0 else vals.at[m, RING, w, pl.ds(row, rows)]
        for place in (1, 2):
            dst = vals.at[m, q * RING + place, w, pl.ds(row, rows)]
            send(("y", q, piece, place), src, dst, to_y[place])

    def y_forward(q, piece, place):
        w, m, row, rows, _ = PIECES[piece]
        half = pl.ds(row + (place - 1) * (rows // 2), rows // 2)
        send(
            ("y", q, piece, 3, place),
            vals.at[m, q * RING + place, w, half],
            vals.at[m, q * RING + 3, w, half],
            to_y[place],
        )

    def v_direct(piece, place):
        w, m, row, rows, _ = PIECES[piece]
        src = own_val(piece) if place == 0 else vals.at[m, place, w, pl.ds(row, rows)]
        send(("v", piece, place), src, vals.at[m, RING + place, w, pl.ds(row, rows)], to_twin)

    def own_ready(piece):
        if piece not in EARLY:
            v_direct(piece, 0)
        y_direct(0, piece)

    def have(q, piece, place):
        first = PIECES[piece][4]
        if first == "y" and q == 0 and place > 0:
            v_direct(piece, place)
        if first == "v" and q == 1 and place == 0:
            y_direct(1, piece)

    def blocks_of(keys):
        return [b for key in keys for b in BLOCKS[key]]

    starts, rows = {}, {}
    for event in ORDER:
        if event[0] == "s1":
            size = len(blocks_of(event[1])) * len(PLACES[event[2]]) * (1 + event[3] // 2)
            first = sum(n for _, n in starts.values())
            rows[event[1:]] = (first * seq_len + 16 * len(starts), size * seq_len + 16)
            starts[event[1:]] = (first, size)

    def act_product(group):
        blocks, places, w = blocks_of(group[0]), PLACES[group[1]], group[2]
        first, size = starts[group]
        n = len(blocks)
        slots = range(1 + w // 2)

        def one(i, carry):
            right = vals[0, places[0] + i, w] if w < 2 else vals[0, places[0] + i].reshape(2 * seq_len, -1)
            part = lax.dot_general(
                trains[0, 2 * blocks[0] : 2 * blocks[0] + 2 * n].reshape(2 * n * seq_len, -1),
                right,
                (((1,), (1,)), ((), ())),
                preferred_element_type=jnp.float32,
            )
            for k in range(n):
                for r in range(2):
                    at_row = (2 * k + r) * seq_len
                    for j in slots:
                        unit = first + (i * n + k) * len(slots) + j
                        acts[r, unit] = part[at_row : at_row + seq_len, j * seq_len : (j + 1) * seq_len]
            return carry

        lax.fori_loop(0, len(places), one, 0)
        send(("s1",) + group, acts.at[1 - core, pl.ds(first, size)], from_core.at[pl.ds(first, size)], to_core)

    def act_cores(group):
        first, size = starts[group]
        row, n_rows = rows[group]
        got(("s1",) + group)

        def add(i, peak):
            value = acts[core, first + i] + from_core[first + i]
            acts[core, first + i] = value
            return jnp.maximum(peak, jnp.max(jnp.abs(value).reshape(seq_len // 8, 8, seq_len), axis=0))

        peak = lax.fori_loop(0, size, add, jnp.zeros((8, seq_len), jnp.float32))
        peak = jnp.max(jnp.max(peak, axis=0, keepdims=True), axis=1, keepdims=True)
        scale = jnp.broadcast_to(jnp.maximum(peak, 1e-30) * 1.01, (16, seq_len)).astype(jnp.bfloat16)
        coded_out[pl.ds(row + size * seq_len, 16)] = scale
        inverse = PEAK / scale.astype(jnp.float32)[0:1]

        def code(i, carry):
            value = acts[core, first + i]
            power = jnp.abs(value) * inverse
            for _ in range(4):
                power = power * power
            power = jnp.where(value < 0, -power, power).astype(jnp.bfloat16)
            coded_out[pl.ds(pl.multiple_of(row + i * seq_len, 16), seq_len)] = power
            return carry

        lax.fori_loop(0, size, code, 0)
        send(("s2",) + group, coded_out.at[pl.ds(row, n_rows)], coded_in.at[pl.ds(row, n_rows)], to_lo)

    def act_whole(group):
        first, size = starts[group]
        row, _ = rows[group]
        got(("s2",) + group)
        scale = coded_in[pl.ds(row + size * seq_len, 16)].astype(jnp.float32)[0:1] * (1.0 / PEAK)

        def one(i, carry):
            power = coded_in[pl.ds(pl.multiple_of(row + i * seq_len, 16), seq_len)].astype(jnp.float32)
            size_of = jnp.abs(power)
            value = jnp.exp(jnp.log(size_of) * (1.0 / POWER)) * scale
            value = jnp.where(power < 0, -value, value)
            whole[core, first + i] = acts[core, first + i] + jnp.where(size_of > 0, value, 0.0)
            return carry

        lax.fori_loop(0, size, one, 0)
        here = whole.at[core, pl.ds(first, size)]
        send(("s3",) + group, here, here, to_core)

    arrived_acts = set()

    def grad_product(b_keys, p_key):
        acts_of = {}
        for b_key in b_keys:
            for group in starts:
                if b_key in group[0] and p_key == group[1]:
                    if group not in arrived_acts:
                        arrived_acts.add(group)
                        got(("s3",) + group)
                    for w in range(2):
                        if group[2] in (w, 2):
                            acts_of[b_key, w] = group

        def one(b_key, i):
            blocks, places = BLOCKS[b_key], PLACES[p_key]
            v, b = places[0] + i // len(blocks), blocks[0] + i % len(blocks)
            add_up(b_key, i, v, b, grads(2 * b, 2, v))

        def grads(train, count, v):
            return lax.dot_general(
                trains[1, pl.ds(train, count)].reshape(count * seq_len, -1),
                vals[1, v].reshape(2 * seq_len, -1),
                (((1,), (1,)), ((), ())),
                preferred_element_type=jnp.float32,
            )

        def add_up(b_key, i, v, b, part):
            blocks = BLOCKS[b_key]
            for w in range(2):
                group = acts_of[b_key, w]
                in_group = blocks_of(group[0])
                unit = i // len(blocks) * len(in_group) + b - in_group[0]
                if group[2] == 2:
                    unit = 2 * unit + w
                unit = starts[group][0] + unit
                for r in range(2):
                    grad = part[r * seq_len : (r + 1) * seq_len, w * seq_len : (w + 1) * seq_len]
                    total = jnp.sum(whole[r, unit] * grad, axis=0, keepdims=True)
                    sums[b // 2, v, w, pl.ds(2 * (b % 2) + r, 1)] = total

        if p_key == LAST and len(blocks_of(b_keys)) == 2:
            (v,), first = PLACES[p_key], blocks_of(b_keys)[0]
            part = grads(2 * first, 4, v)
            for b_key in b_keys:
                for i, b in enumerate(BLOCKS[b_key]):
                    row = (b - first) * 2 * seq_len
                    add_up(b_key, i, v, b, part[row : row + 2 * seq_len])
            return
        for b_key in b_keys:
            count = len(BLOCKS[b_key]) * len(PLACES[p_key])
            lax.fori_loop(0, count, lambda i, carry: (one(b_key, i), carry)[1], 0)

    group_of = ((z_lo, core), (z_lo, 1 - core), (1 - z_lo, core), (1 - z_lo, 1 - core))

    lane = lax.broadcasted_iota(jnp.int32, (4, 128), 1)

    def fold(side, p_keys):
        for v in [v for p_key in p_keys for v in PLACES[p_key]]:
            for w in range(2):
                its_z_hi = z_hi if w == 0 else 1 - z_hi
                column = its_z_hi * 16 + y_at[v % RING] * 4 + (x if v < RING else twin)
                total = jnp.sum(sums[side, v, w], axis=1, keepdims=True)
                scores[side] = jnp.where(lane == column, total, scores[side])

    def out(side):
        tiles[side, 0:4] = scores[side] * (1.0 / (total_width * seq_len))
        for d in (3, 2, 1, 0):
            its_z_lo, its_core = group_of[d]
            if (side, d) != (0, 0):
                device = at(z_hi, y, (x, mate)[side], its_z_lo, its_core)
                send(("out", side, d), tiles.at[side], arrived.at[side, d], device)

    half_a, half_b = pl.ds(0, seq_len // 2), pl.ds(seq_len // 2, seq_len // 2)
    def pass_on(m):
        send(("ra", m), val_in[m].at[0, half_a], relay.at[0, m], to_lo)
        send(("rb", m), val_in[m].at[0, half_b], relay.at[1, m], to_hi)

    for piece in AT_ONCE:
        own_ready(piece)
    for m in range(2):
        pass_on(m)
    for piece in EARLY:
        v_direct(piece, 0)
    for m in range(2):
        for h in range(2):
            send(("x", m, h), train_in[m].at[pl.ds(2 * h, 2)], trains.at[m, pl.ds(4 + 2 * h, 2)], to_mate)
    for copy in local:
        copy.wait()

    seen = set()
    scores = [jnp.zeros((4, 128), jnp.float32)] * 2
    for event in ORDER:
        kind = event[0]
        if kind == "go":
            own_ready(*event[1:])
            continue
        if kind.startswith("fold"):
            for side in range(2):
                if kind != ("fold1", "fold0")[side]:
                    fold(side, event[1:])
            continue
        if kind == "out":
            out(event[1])
            continue
        if kind == "s1":
            act_product(event[1:])
            continue
        if kind == "s2":
            act_cores(event[1:])
            continue
        if kind == "s3":
            act_whole(event[1:])
            continue
        if kind == "s4":
            grad_product(*event[1:])
            continue
        got(event)
        if kind == "ra":
            m = event[1]
            send(("fa", m), relay.at[0, m], vals.at[m, 0, 1, half_a], to_hi)
        elif kind == "rb":
            m = event[1]
            send(("fb", m), relay.at[1, m], vals.at[m, 0, 1, half_b], to_lo)
        elif kind == "v":
            have(1, *event[1:])
        elif kind == "y":
            q, piece, place = event[1:4]
            if place < 3:
                y_forward(q, piece, place)
                have(q, piece, place)
            elif event[:4] in seen:
                have(q, piece, place)
            seen.add(event[:4])
    total = tiles[0, 0:4]
    for side in range(2):
        for d in range(4):
            if (side, d) != (0, 0):
                got(("out", side, d))
                total = total + arrived[side, d, 0:4]
    result[...] = total[:, : out_ref.shape[1]]
    copy_out = pltpu.make_async_copy(result, out_ref, local_sem.at[0])
    copy_out.start()
    for copy in copies.values():
        copy.wait_send()
    copy_out.wait()


GROUPS = sum(1 for event in ORDER if event[0] == "s1")
UNITS = 2 * 4 * 2 * RING
Y_RINGS = sum(1 if first == "y" else 2 for *_, first in PIECES)
V_COPIES = sum(RING if first == "y" else 1 for *_, first in PIECES)
N_COPIES = 8 + 4 + 4 * Y_RINGS + V_COPIES + 3 * GROUPS + 7


def per_device(train_act, train_grad, val_act, val_grad):
    n_train, seq_len, width = train_act.shape
    n_val = lax.axis_size("dp")
    bf16, f32 = train_act.dtype, jnp.float32
    anywhere = pl.BlockSpec(memory_space=pl.ANY)
    coded = (UNITS * seq_len + 16 * GROUPS, seq_len)
    return pl.pallas_call(
        functools.partial(kernel, width * lax.axis_size("tensor")),
        out_shape=jax.ShapeDtypeStruct((n_train, n_val), f32),
        in_specs=[anywhere] * 4,
        out_specs=anywhere,
        scratch_shapes=[
            pltpu.VMEM((2, 2 * n_train, seq_len, width), bf16),
            pltpu.VMEM((2, 2 * RING, 2, seq_len, width), bf16),
            pltpu.VMEM((2, 2, seq_len // 2, width), bf16),
            pltpu.VMEM((2, UNITS, seq_len, seq_len), f32),
            pltpu.VMEM((UNITS, seq_len, seq_len), f32),
            pltpu.VMEM(coded, bf16),
            pltpu.VMEM(coded, bf16),
            pltpu.VMEM((2, UNITS, seq_len, seq_len), f32),
            pltpu.VMEM((2, 2 * RING, 2, 4, seq_len), f32),
            pltpu.VMEM((2, 8, 128), f32),
            pltpu.VMEM((2, 4, 8, 128), f32),
            pltpu.VMEM((n_train, n_val), f32),
            pltpu.SemaphoreType.DMA((4,)),
            pltpu.SemaphoreType.DMA((N_COPIES,)),
            pltpu.SemaphoreType.DMA((N_COPIES,)),
        ],
        compiler_params=pltpu.CompilerParams(
            collective_id=0, has_side_effects=True, vmem_limit_bytes=56 * 1024 * 1024
        ),
        cost_estimate=pl.CostEstimate(
            flops=4 * 32 * (2 * seq_len) ** 2 * width, bytes_accessed=3_300_000, transcendentals=0
        ),
    )(train_act, train_grad, val_act, val_grad)


def solution(mesh):
    placed = P("dp", None, "tensor")
    return jax.shard_map(
        per_device, mesh=mesh, in_specs=(placed,) * 4, out_specs=P("dp", None), check_vma=False
    )
```

```python
import functools

import jax
import jax.numpy as jnp
from jax import lax
from jax.experimental import pallas as pl
from jax.experimental.pallas import tpu as pltpu
from jax.sharding import PartitionSpec as P

MESH = pl.DeviceIdType.MESH
LAST = "f"
RING = 4

BLOCKS = {"o": (0, 1), "p": (2,), "s": (3,)}
PLACES = {"a": (0,), "b": (1, 2), "c": (3,), "d": (4,), "e": (5, 6), "f": (7,)}

PIECES = (
    (0, 0, 0, 64, "v"),
    (0, 0, 64, 64, "y"),
    (1, 0, 0, 128, "v"),
    (0, 1, 0, 32, "y"),
    (0, 1, 32, 96, "y"),
    (1, 1, 0, 32, "y"),
    (1, 1, 32, 96, "v"),
)
AT_ONCE = (0, 1)

EARLY = (3,)
ORDER = (
    ("v", 0, 0), ("y", 0, 0, 1), ("y", 0, 0, 2), ("ra", 0), ("rb", 0), ("go", 3), ("s1", "o", "a", 0),
    ("v", 1, 0), ("y", 0, 1, 1), ("y", 0, 1, 2), ("ra", 1), ("rb", 1), ("s1", "o", "b", 0), ("v", 3, 0),
    ("s2", "o", "a", 0), ("s1", "o", "d", 0), ("y", 1, 0, 1), ("y", 1, 0, 2), ("fa", 0), ("fb", 0), ("go", 2),
    ("s1", "o", "a", 1), ("s2", "o", "b", 0), ("y", 0, 0, 3, 1), ("y", 0, 0, 3, 2), ("s2", "o", "d", 0),
    ("v", 1, 1), ("x", 0, 0), ("s1", "p", "a", 2), ("fa", 1), ("fb", 1), ("go", 5), ("y", 0, 3, 1),
    ("y", 0, 3, 2), ("s2", "o", "a", 1), ("s1", "p", "b", 0), ("s3", "o", "a", 0), ("s1", "p", "d", 0),
    ("y", 0, 1, 3, 1), ("y", 0, 1, 3, 2), ("s1", "op", "c", 0), ("v", 1, 2), ("s2", "p", "a", 2),
    ("s1", "op", "e", 0), ("y", 1, 0, 3, 1), ("y", 1, 0, 3, 2), ("s2", "p", "b", 0), ("s2", "p", "d", 0),
    ("s3", "o", "b", 0), ("s2", "op", "c", 0), ("s3", "o", "d", 0), ("s3", "o", "a", 1), ("s2", "op", "e", 0),
    ("s3", "p", "a", 2), ("v", 2, 0), ("s1", "op", "d", 1), ("y", 0, 2, 1), ("y", 0, 2, 2),
    ("s3", "p", "b", 0), ("s1", "op", "b", 1), ("v", 5, 0), ("y", 0, 5, 1), ("y", 0, 5, 2), ("go", 4),
    ("y", 0, 3, 3, 1), ("y", 0, 3, 3, 2), ("v", 3, 1), ("x", 0, 1), ("s2", "op", "d", 1), ("s3", "p", "d", 0),
    ("s3", "op", "c", 0), ("s1", "s", "a", 2), ("s1", "s", "b", 2), ("v", 3, 2), ("s1", "s", "c", 0),
    ("s1", "s", "d", 2), ("s2", "op", "b", 1), ("s4", "o", "a"), ("s2", "s", "a", 2), ("s3", "op", "e", 0),
    ("s2", "s", "b", 2), ("s2", "s", "c", 0), ("v", 1, 3), ("s2", "s", "d", 2), ("s3", "op", "d", 1),
    ("y", 1, 2, 1), ("y", 1, 2, 2), ("v", 5, 1), ("s1", "s", "e", 2), ("s1", "op", "e", 1), ("v", 5, 2),
    ("y", 0, 2, 3, 1), ("go", 6), ("y", 0, 2, 3, 2), ("s1", "ops", "c", 1), ("y", 0, 5, 3, 1),
    ("y", 0, 5, 3, 2), ("s2", "s", "e", 2), ("s3", "op", "b", 1), ("s2", "op", "e", 1), ("s3", "s", "a", 2),
    ("x", 1, 0), ("s4", "p", "a"), ("v", 4, 0), ("s2", "ops", "c", 1), ("s3", "s", "b", 2), ("v", 3, 3),
    ("s3", "s", "c", 0), ("y", 0, 4, 1), ("y", 0, 4, 2), ("s3", "s", "d", 2), ("y", 1, 2, 3, 1),
    ("y", 1, 2, 3, 2), ("s1", "o", "f", 2), ("s1", "p", "f", 2), ("s3", "s", "e", 2), ("v", 6, 0),
    ("s1", "s", "f", 2), ("s4", "o", "d"), ("s4", "p", "d"), ("v", 5, 3), ("s2", "o", "f", 2),
    ("s2", "p", "f", 2), ("s2", "s", "f", 2), ("s3", "op", "e", 1), ("y", 0, 6, 1), ("y", 0, 6, 2),
    ("s4", "o", "b"), ("s4", "p", "b"), ("x", 1, 1), ("y", 0, 4, 3, 1), ("y", 0, 4, 3, 2), ("v", 4, 1),
    ("s3", "ops", "c", 1), ("s4", "s", "a"), ("fold", "a"), ("s4", "s", "b"), ("fold", "b"), ("s4", "s", "d"),
    ("fold", "d"), ("s3", "o", "f", 2), ("s3", "p", "f", 2), ("y", 1, 6, 1), ("y", 1, 6, 2), ("v", 4, 2),
    ("s4", "o", "e"), ("s3", "s", "f", 2), ("s4", "p", "e"), ("y", 0, 6, 3, 1), ("y", 0, 6, 3, 2),
    ("s4", "o", "c"), ("s4", "p", "c"), ("s4", "s", "c"), ("s4", "s", "e"), ("y", 1, 6, 3, 1), ("v", 4, 3),
    ("y", 1, 6, 3, 2), ("fold", "c", "e"), ("s4", "ps", "f"), ("fold1", "f"), ("out", 1), ("s4", "o", "f"),
    ("fold0", "f"), ("out", 0),
)

POWER = 16
PEAK = 222.0


def kernel(
    total_width,
    train_act,
    train_grad,
    val_act,
    val_grad,
    out_ref,
    trains,
    vals,
    relay,
    acts,
    from_core,
    coded_out,
    coded_in,
    whole,
    sums,
    tiles,
    arrived,
    result,
    local_sem,
    send_sem,
    recv_sem,
):
    seq_len = train_act.shape[1]
    train_in = (train_act, train_grad)
    val_in = (val_act, val_grad)

    dp = lax.axis_index("dp")
    tensor = lax.axis_index("tensor")
    z_hi, y, x = dp // 16, (dp // 4) % 4, dp % 4
    z_lo, core = tensor // 2, tensor % 2

    def at(z_hi, y, x, z_lo, core):
        return (z_hi * 16 + y * 4 + x, z_lo * 2 + core)

    mate, twin = x + 1 - 2 * (x % 2), 3 - x
    y_at = (y, (y + 3) % 4, (y + 1) % 4, (y + 2) % 4)
    to_y = {1: at(z_hi, y_at[2], x, z_lo, core), 2: at(z_hi, y_at[1], x, z_lo, core)}
    to_mate = at(z_hi, y, mate, z_lo, core)
    to_twin = at(z_hi, y, twin, z_lo, core)
    to_lo = at(z_hi, y, x, 1 - z_lo, core)
    to_hi = at(1 - z_hi, y, x, 1 - z_lo, core)
    to_core = at(z_hi, y, x, z_lo, 1 - core)

    local = []
    for m in range(2):
        local.append(
            pltpu.make_async_copy(train_in[m], trains.at[m, pl.ds(0, 4)], local_sem.at[m])
        )
        local.append(
            pltpu.make_async_copy(val_in[m], vals.at[m, 0, pl.ds(0, 1)], local_sem.at[2 + m])
        )
    for copy in local:
        copy.start()

    barrier = pltpu.get_barrier_semaphore()
    partners = [to_mate, to_twin, to_y[1], to_y[2], to_lo, to_hi, to_core]
    for device in partners:
        pl.semaphore_signal(barrier, inc=1, device_id=device, device_id_type=MESH)
    pl.semaphore_wait(barrier, len(partners))

    copies = {}

    def send(name, src, dst, device):
        key = len(copies)
        copies[name] = pltpu.make_async_remote_copy(
            src_ref=src,
            dst_ref=dst,
            send_sem=send_sem.at[key],
            recv_sem=recv_sem.at[key],
            device_id=device,
            device_id_type=MESH,
        )
        copies[name].start()

    def got(name):
        copies[name].wait_recv()

    def own_val(piece):
        w, m, row, rows, _ = PIECES[piece]
        rows = pl.ds(row, rows)
        return val_in[m].at[0, rows] if w == 0 else vals.at[m, 0, 1, rows]

    def y_direct(q, piece):
        w, m, row, rows, _ = PIECES[piece]
        src = own_val(piece) if q == 0 else vals.at[m, RING, w, pl.ds(row, rows)]
        for place in (1, 2):
            dst = vals.at[m, q * RING + place, w, pl.ds(row, rows)]
            send(("y", q, piece, place), src, dst, to_y[place])

    def y_forward(q, piece, place):
        w, m, row, rows, _ = PIECES[piece]
        half = pl.ds(row + (place - 1) * (rows // 2), rows // 2)
        send(
            ("y", q, piece, 3, place),
            vals.at[m, q * RING + place, w, half],
            vals.at[m, q * RING + 3, w, half],
            to_y[place],
        )

    def v_direct(piece, place):
        w, m, row, rows, _ = PIECES[piece]
        src = own_val(piece) if place == 0 else vals.at[m, place, w, pl.ds(row, rows)]
        send(("v", piece, place), src, vals.at[m, RING + place, w, pl.ds(row, rows)], to_twin)

    def own_ready(piece):
        if piece not in EARLY:
            v_direct(piece, 0)
        y_direct(0, piece)

    def have(q, piece, place):
        first = PIECES[piece][4]
        if first == "y" and q == 0 and place > 0:
            v_direct(piece, place)
        if first == "v" and q == 1 and place == 0:
            y_direct(1, piece)

    def blocks_of(keys):
        return [b for key in keys for b in BLOCKS[key]]

    starts, rows = {}, {}
    for event in ORDER:
        if event[0] == "s1":
            size = len(blocks_of(event[1])) * len(PLACES[event[2]]) * (1 + event[3] // 2)
            first = sum(n for _, n in starts.values())
            rows[event[1:]] = (first * seq_len + 16 * len(starts), size * seq_len + 16)
            starts[event[1:]] = (first, size)

    def act_product(group):
        blocks, places, w = blocks_of(group[0]), PLACES[group[1]], group[2]
        first, size = starts[group]
        n = len(blocks)
        slots = range(1 + w // 2)

        def one(i, carry):
            right = vals[0, places[0] + i, w] if w < 2 else vals[0, places[0] + i].reshape(2 * seq_len, -1)
            part = lax.dot_general(
                trains[0, 2 * blocks[0] : 2 * blocks[0] + 2 * n].reshape(2 * n * seq_len, -1),
                right,
                (((1,), (1,)), ((), ())),
                preferred_element_type=jnp.float32,
            )
            for k in range(n):
                for r in range(2):
                    at_row = (2 * k + r) * seq_len
                    for j in slots:
                        unit = first + (i * n + k) * len(slots) + j
                        acts[r, unit] = part[at_row : at_row + seq_len, j * seq_len : (j + 1) * seq_len]
            return carry

        lax.fori_loop(0, len(places), one, 0)
        send(("s1",) + group, acts.at[1 - core, pl.ds(first, size)], from_core.at[pl.ds(first, size)], to_core)

    def act_cores(group):
        first, size = starts[group]
        row, n_rows = rows[group]
        got(("s1",) + group)

        def add(i, peak):
            value = acts[core, first + i] + from_core[first + i]
            acts[core, first + i] = value
            return jnp.maximum(peak, jnp.max(jnp.abs(value).reshape(seq_len // 8, 8, seq_len), axis=0))

        peak = lax.fori_loop(0, size, add, jnp.zeros((8, seq_len), jnp.float32))
        peak = jnp.max(jnp.max(peak, axis=0, keepdims=True), axis=1, keepdims=True)
        scale = jnp.broadcast_to(jnp.maximum(peak, 1e-30) * 1.01, (16, seq_len)).astype(jnp.bfloat16)
        coded_out[pl.ds(row + size * seq_len, 16)] = scale
        inverse = PEAK / scale.astype(jnp.float32)[0:1]

        def code(i, carry):
            value = acts[core, first + i]
            power = jnp.abs(value) * inverse
            for _ in range(4):
                power = power * power
            power = jnp.where(value < 0, -power, power).astype(jnp.bfloat16)
            coded_out[pl.ds(pl.multiple_of(row + i * seq_len, 16), seq_len)] = power
            return carry

        lax.fori_loop(0, size, code, 0)
        send(("s2",) + group, coded_out.at[pl.ds(row, n_rows)], coded_in.at[pl.ds(row, n_rows)], to_lo)

    def act_whole(group):
        first, size = starts[group]
        row, _ = rows[group]
        got(("s2",) + group)
        scale = coded_in[pl.ds(row + size * seq_len, 16)].astype(jnp.float32)[0:1] * (1.0 / PEAK)

        def one(i, carry):
            power = coded_in[pl.ds(pl.multiple_of(row + i * seq_len, 16), seq_len)].astype(jnp.float32)
            size_of = jnp.abs(power)
            value = jnp.exp(jnp.log(size_of) * (1.0 / POWER)) * scale
            value = jnp.where(power < 0, -value, value)
            whole[core, first + i] = acts[core, first + i] + jnp.where(size_of > 0, value, 0.0)
            return carry

        lax.fori_loop(0, size, one, 0)
        here = whole.at[core, pl.ds(first, size)]
        send(("s3",) + group, here, here, to_core)

    arrived_acts = set()

    def grad_product(b_keys, p_key):
        acts_of = {}
        for b_key in b_keys:
            for group in starts:
                if b_key in group[0] and p_key == group[1]:
                    if group not in arrived_acts:
                        arrived_acts.add(group)
                        got(("s3",) + group)
                    for w in range(2):
                        if group[2] in (w, 2):
                            acts_of[b_key, w] = group

        def one(b_key, i):
            blocks, places = BLOCKS[b_key], PLACES[p_key]
            v, b = places[0] + i // len(blocks), blocks[0] + i % len(blocks)
            part = lax.dot_general(
                trains[1, pl.ds(2 * b, 2)].reshape(2 * seq_len, -1),
                vals[1, v].reshape(2 * seq_len, -1),
                (((1,), (1,)), ((), ())),
                preferred_element_type=jnp.float32,
            )
            for w in range(2):
                group = acts_of[b_key, w]
                in_group = blocks_of(group[0])
                unit = i // len(blocks) * len(in_group) + b - in_group[0]
                if group[2] == 2:
                    unit = 2 * unit + w
                unit = starts[group][0] + unit
                for r in range(2):
                    grad = part[r * seq_len : (r + 1) * seq_len, w * seq_len : (w + 1) * seq_len]
                    total = jnp.sum(whole[r, unit] * grad, axis=0, keepdims=True)
                    sums[b // 2, v, w, pl.ds(2 * (b % 2) + r, 1)] = total

        for b_key in b_keys:
            count = len(BLOCKS[b_key]) * len(PLACES[p_key])
            if p_key == LAST:
                for i in range(count):
                    one(b_key, i)
            else:
                lax.fori_loop(0, count, lambda i, carry: (one(b_key, i), carry)[1], 0)

    group_of = ((z_lo, core), (z_lo, 1 - core), (1 - z_lo, core), (1 - z_lo, 1 - core))

    lane = lax.broadcasted_iota(jnp.int32, (4, 128), 1)

    def fold(side, p_keys):
        for v in [v for p_key in p_keys for v in PLACES[p_key]]:
            for w in range(2):
                its_z_hi = z_hi if w == 0 else 1 - z_hi
                column = its_z_hi * 16 + y_at[v % RING] * 4 + (x if v < RING else twin)
                total = jnp.sum(sums[side, v, w], axis=1, keepdims=True)
                scores[side] = jnp.where(lane == column, total, scores[side])

    def out(side):
        tiles[side, 0:4] = scores[side] * (1.0 / (total_width * seq_len))
        for d in (3, 2, 1, 0):
            its_z_lo, its_core = group_of[d]
            if (side, d) != (0, 0):
                device = at(z_hi, y, (x, mate)[side], its_z_lo, its_core)
                send(("out", side, d), tiles.at[side], arrived.at[side, d], device)

    half_a, half_b = pl.ds(0, seq_len // 2), pl.ds(seq_len // 2, seq_len // 2)
    def pass_on(m):
        send(("ra", m), val_in[m].at[0, half_a], relay.at[0, m], to_lo)
        send(("rb", m), val_in[m].at[0, half_b], relay.at[1, m], to_hi)

    pass_on(0)
    for piece in AT_ONCE:
        own_ready(piece)
    pass_on(1)
    for piece in EARLY:
        v_direct(piece, 0)
    for m in range(2):
        for h in range(2):
            send(("x", m, h), train_in[m].at[pl.ds(2 * h, 2)], trains.at[m, pl.ds(4 + 2 * h, 2)], to_mate)
    for copy in local:
        copy.wait()

    seen = set()
    scores = [jnp.zeros((4, 128), jnp.float32)] * 2
    for event in ORDER:
        kind = event[0]
        if kind == "go":
            own_ready(*event[1:])
            continue
        if kind.startswith("fold"):
            for side in range(2):
                if kind != ("fold1", "fold0")[side]:
                    fold(side, event[1:])
            continue
        if kind == "out":
            out(event[1])
            continue
        if kind == "s1":
            act_product(event[1:])
            continue
        if kind == "s2":
            act_cores(event[1:])
            continue
        if kind == "s3":
            act_whole(event[1:])
            continue
        if kind == "s4":
            grad_product(*event[1:])
            continue
        got(event)
        if kind == "ra":
            m = event[1]
            send(("fa", m), relay.at[0, m], vals.at[m, 0, 1, half_a], to_hi)
        elif kind == "rb":
            m = event[1]
            send(("fb", m), relay.at[1, m], vals.at[m, 0, 1, half_b], to_lo)
        elif kind == "v":
            have(1, *event[1:])
        elif kind == "y":
            q, piece, place = event[1:4]
            if place < 3:
                y_forward(q, piece, place)
                have(q, piece, place)
            elif event[:4] in seen:
                have(q, piece, place)
            seen.add(event[:4])
    total = tiles[0, 0:4]
    for side in range(2):
        for d in range(4):
            if (side, d) != (0, 0):
                got(("out", side, d))
                total = total + arrived[side, d, 0:4]
    result[...] = total[:, : out_ref.shape[1]]
    copy_out = pltpu.make_async_copy(result, out_ref, local_sem.at[0])
    copy_out.start()
    for copy in copies.values():
        copy.wait_send()
    copy_out.wait()


GROUPS = sum(1 for event in ORDER if event[0] == "s1")
UNITS = 2 * 4 * 2 * RING
Y_RINGS = sum(1 if first == "y" else 2 for *_, first in PIECES)
V_COPIES = sum(RING if first == "y" else 1 for *_, first in PIECES)
N_COPIES = 8 + 4 + 4 * Y_RINGS + V_COPIES + 3 * GROUPS + 7


def per_device(train_act, train_grad, val_act, val_grad):
    n_train, seq_len, width = train_act.shape
    n_val = lax.axis_size("dp")
    bf16, f32 = train_act.dtype, jnp.float32
    anywhere = pl.BlockSpec(memory_space=pl.ANY)
    coded = (UNITS * seq_len + 16 * GROUPS, seq_len)
    return pl.pallas_call(
        functools.partial(kernel, width * lax.axis_size("tensor")),
        out_shape=jax.ShapeDtypeStruct((n_train, n_val), f32),
        in_specs=[anywhere] * 4,
        out_specs=anywhere,
        scratch_shapes=[
            pltpu.VMEM((2, 2 * n_train, seq_len, width), bf16),
            pltpu.VMEM((2, 2 * RING, 2, seq_len, width), bf16),
            pltpu.VMEM((2, 2, seq_len // 2, width), bf16),
            pltpu.VMEM((2, UNITS, seq_len, seq_len), f32),
            pltpu.VMEM((UNITS, seq_len, seq_len), f32),
            pltpu.VMEM(coded, bf16),
            pltpu.VMEM(coded, bf16),
            pltpu.VMEM((2, UNITS, seq_len, seq_len), f32),
            pltpu.VMEM((2, 2 * RING, 2, 4, seq_len), f32),
            pltpu.VMEM((2, 8, 128), f32),
            pltpu.VMEM((2, 4, 8, 128), f32),
            pltpu.VMEM((n_train, n_val), f32),
            pltpu.SemaphoreType.DMA((4,)),
            pltpu.SemaphoreType.DMA((N_COPIES,)),
            pltpu.SemaphoreType.DMA((N_COPIES,)),
        ],
        compiler_params=pltpu.CompilerParams(
            collective_id=0, has_side_effects=True, vmem_limit_bytes=56 * 1024 * 1024
        ),
        cost_estimate=pl.CostEstimate(
            flops=4 * 32 * (2 * seq_len) ** 2 * width, bytes_accessed=3_300_000, transcendentals=0
        ),
    )(train_act, train_grad, val_act, val_grad)


def solution(mesh):
    placed = P("dp", None, "tensor")
    return jax.shard_map(
        per_device, mesh=mesh, in_specs=(placed,) * 4, out_specs=P("dp", None), check_vma=False
    )
```
